256 devices in a mesh: site: 16 (over z, core), sector: 16 (over y, x).
Axes of the slice: x: 4, y: 4, z: 8, core: 2. Of those that a mesh axis runs over, the one named last changes fastest.
Arguments:
- site_tensor: float32 [16, 4, 16, 512, 512], P('site', None, 'sector'), may hold values from -0.25 to 0.25
- outcomes: int32 [6, 16, 128], P(None, 'site'), may hold values from 0 to 3
- in_flight: float32 [16, 128, 8192], P('site', None, 'sector'), may hold values from -6 to 6
- prior_logp: float32 [16, 128], P('site'), may hold values from -30 to 0
- entering: float32 [5, 128, 8192], P(None, None, 'sector'), may hold values from -6 to 6
Outputs:
- final_env: float32 [16, 128, 8192], P('site', None, 'sector')
- final_logp: float32 [16, 128], P('site')
The draws below stay inside these ranges and needn't reach their ends.
All inputs are finite; a program needn't handle non-finite values.
Results may differ from the reference program's by a relative error of at most 0.0003.
Values sent between devices are 32-bit elements; how exact they have to be, the bound alone decides.
A program may use at most 64 MiB of HBM per device.

```python
import jax
import jax.numpy as jnp
from jax import lax

SECTORS = 16
SEC = 512
OUTCOMES = 4
ROWS = 128
TICKS = 6
BOND = 8192
SITES = 16
ENTERING = 5


def plant(array, own_key, smallest, high):
    longest = array.shape.index(max(array.shape))
    spots = []
    for shift in (0, 1):
        where = [jax.random.randint(jax.random.fold_in(own_key, axis), (), 0, length) for axis, length in enumerate(array.shape)]
        where[longest] = (where[longest] + shift) % array.shape[longest]
        spots.append(tuple(where))
    return array.at[spots[0]].set(smallest).at[spots[1]].set(high)


def block_levels(rng, shape, cuts, low, top_value):
    factor_of, own = 1.0, jax.random.fold_in(rng, 6)
    for axis_at, shards_of in cuts:
        draws = jnp.exp(jax.random.uniform(jax.random.fold_in(own, axis_at), (shards_of,), jnp.float32, low / len(cuts), top_value / len(cuts)))
        factor_of = factor_of * jnp.repeat(draws, shape[axis_at] // shards_of).reshape([-1 if axis == axis_at else 1 for axis in range(len(shape))])
    return factor_of


def noise(key, dims, deviation, most, pieces=(), held_as=jnp.bfloat16):
    entries = deviation * jax.random.normal(key, dims, jnp.float32)
    if pieces:
        entries = entries * block_levels(key, dims, pieces, -0.22, 0.18)
    return jnp.clip(entries, -most, most).astype(held_as)


def setup_inputs(seed: int = 0) -> dict:
    key_list = jax.random.split(jax.random.key(seed), 6)
    site_tensor = noise(key_list[0], (SITES, OUTCOMES, SECTORS, SEC, SEC), SEC ** -0.5, 0.25, ((0, 16), (2, 16)), jnp.float32)
    outcomes = plant(jax.random.randint(key_list[1], (TICKS, SITES, ROWS), 0, OUTCOMES), jax.random.fold_in(key_list[1], 1), 0, OUTCOMES - 1).astype(jnp.int32)
    in_flight = noise(key_list[2], (SITES, ROWS, BOND), 1.0, 6.0, ((0, 16), (2, 16)), jnp.float32)
    prior_logp = jnp.clip(-30.0 + 30.0 * jax.random.uniform(key_list[3], (SITES, ROWS), jnp.float32) ** block_levels(key_list[3], (SITES, ROWS), ((0, 16),), -0.2, 0.2), -30.0, 0.0)
    entering = noise(key_list[4], (ENTERING, ROWS, BOND), 1.0, 6.0, ((2, 16),), jnp.float32)
    return dict(site_tensor=site_tensor, outcomes=outcomes, in_flight=in_flight, prior_logp=prior_logp, entering=entering)


EPSILON = 1e-06

def reference(site_tensor, outcomes, in_flight, prior_logp, entering):

    def one_site(operands):
        tensor, states, log_weight, chosen = operands
        blocks = states.reshape(ROWS, SECTORS, SEC)
        padded = jnp.concatenate([blocks, jnp.zeros((ROWS, OUTCOMES - 1, SEC), dtype=states.dtype)], axis=1)
        picked = jnp.stack([padded[:, count:count + SECTORS] for count in range(OUTCOMES)], axis=1)
        amplitude = jnp.einsum('rnsi,nsij->rnsj', picked, tensor, precision=lax.Precision.HIGHEST)
        amplitude = amplitude.reshape(ROWS, OUTCOMES, BOND)
        power = lax.optimization_barrier(jnp.mean(amplitude * amplitude, axis=2))
        selector = (chosen[:, None] == jnp.arange(OUTCOMES, dtype=jnp.int32)[None, :]).astype(amplitude.dtype)
        picked_mean = lax.optimization_barrier(jnp.sum(power * selector, axis=1)) + EPSILON
        total_mean = lax.optimization_barrier(jnp.sum(power, axis=1)) + EPSILON
        selected = lax.optimization_barrier(jnp.sum(amplitude * selector[:, :, None], axis=1))
        normalized = selected / jnp.sqrt(picked_mean)[:, None]
        return (normalized, log_weight + jnp.log(picked_mean) - jnp.log(total_mean))
    states = in_flight
    log_weight = prior_logp
    for tick_index in range(TICKS):
        if tick_index > 0:
            states = jnp.concatenate([entering[tick_index - 1][None], states[:-1]], axis=0)
            log_weight = jnp.concatenate([jnp.zeros((1, ROWS), dtype=prior_logp.dtype), log_weight[:-1]], axis=0)
        states, log_weight = lax.map(one_site, (site_tensor, states, log_weight, outcomes[tick_index]))
    return (states, log_weight)
```

```python
import functools

import jax
import jax.numpy as jnp
from jax import lax
from jax.experimental import pallas as pl
from jax.experimental.pallas import tpu as pltpu
from jax.sharding import PartitionSpec as P

EPSILON = 1e-06
CHUNKS = 4
LANES = 128
MESH = pl.DeviceIdType.MESH


def when(condition):
    return pl.when(condition)


def lane_and_row(rows):
    lane = lax.broadcasted_iota(jnp.int32, (rows, LANES), 1)
    row = lax.broadcasted_iota(jnp.int32, (rows, LANES), 0)
    return lane, row


def column_of(vector, offset, rows):
    lane, row = lane_and_row(rows)
    spread = jnp.broadcast_to(vector, (rows, LANES))
    return jnp.sum(jnp.where(lane == row + offset, spread, 0.0), axis=1, keepdims=True)


def vector_of(columns, rows):
    lane, row = lane_and_row(rows)
    spread = jnp.zeros((rows, LANES), jnp.float32)
    for offset, column in columns:
        spread = spread + jnp.where(lane == row + offset, column, 0.0)
    return jnp.sum(spread, axis=0, keepdims=True)


def halves(value):
    high = value.astype(jnp.bfloat16)
    return high, (value - high.astype(jnp.float32)).astype(jnp.bfloat16)


def kernel(
    ticks,
    side,
    sites,
    bond,
    site_tensor,
    outcomes,
    in_flight,
    prior,
    entering,
    env_out,
    logp_out,
    raw,
    high,
    low,
    slots,
    picked,
    message,
    along_x,
    along_y,
    raw_sem,
    local_sem,
    slot_sem,
    x_sem,
    y_sem,
    send_sem,
    x_send_sem,
    y_send_sem,
):
    site, sector = lax.axis_index("site"), lax.axis_index("sector")
    x, y = sector % side, sector // side
    sectors = side * side
    last = sectors - 1
    rows = slots.shape[3]

    def local_row(index):
        return pltpu.make_async_copy(
            in_flight.at[0, pl.ds(index * rows, rows), :], slots.at[0, index, 0], slot_sem.at[0, index, 0]
        )

    def local_entering(tick, index):
        return pltpu.make_async_copy(
            entering.at[tick - 1, pl.ds(index * rows, rows), :],
            slots.at[tick, index, 0],
            slot_sem.at[tick, index, 0],
        )

    raw_copies = [
        pltpu.make_async_copy(site_tensor.at[0, count, 0], raw.at[count], raw_sem.at[count]) for count in range(4)
    ]
    for index in range(CHUNKS):
        local_row(index).start()
    for copy in raw_copies:
        copy.start()

    for count in range(1, 4):

        @when(sector + count > last)
        def _():
            def clear(index, carry):
                slots[index // CHUNKS, index % CHUNKS, count] = jnp.zeros((rows, slots.shape[4]), jnp.float32)
                return carry

            lax.fori_loop(0, ticks * CHUNKS, clear, 0)

    along_x[...] = jnp.zeros_like(along_x)
    along_y[...] = jnp.zeros_like(along_y)

    barrier = pltpu.get_barrier_semaphore()

    def greet(condition, where):
        @when(condition)
        def _():
            pl.semaphore_signal(barrier, inc=1, device_id=where, device_id_type=MESH)

    always = site >= 0
    expected = jnp.int32(2 * (side - 1))
    for hop in range(1, side):
        greet(always, (site, y * side + (x + hop) % side))
        greet(always, (site, (y + hop) % side * side + x))
    greet((x == side - 1) & (sector < last), (site, sector + 1))
    expected += ((x == 0) & (sector > 0)).astype(jnp.int32)
    greet((x != 0) & (sector + 3 <= last), (site, sector + 3))
    expected += ((x != side - 1) & (sector >= 3)).astype(jnp.int32)
    greet((x == 0) & (sector > 0), (site, sector - 1))
    expected += ((x == side - 1) & (sector < last)).astype(jnp.int32)
    has_next = site < sites - 1
    for hop in range(side):
        greet(site > 0, (site - 1, y * side + (x + hop) % side))
        expected += has_next.astype(jnp.int32)
    greet((site > 0) & (x == side - 1) & (sector < last), (site - 1, sector + 1))
    expected += (has_next & (x == 0) & (sector > 0)).astype(jnp.int32)
    greet((site > 0) & (x != 0) & (sector + 3 <= last), (site - 1, sector + 3))
    expected += (has_next & (x != side - 1) & (sector >= 3)).astype(jnp.int32)
    pl.semaphore_wait(barrier, expected)

    def remote(source, tick, index, count, kind, where):
        return pltpu.make_async_remote_copy(
            src_ref=source,
            dst_ref=slots.at[tick, index, count],
            send_sem=send_sem.at[kind, tick, index],
            recv_sem=slot_sem.at[tick, index, count],
            device_id=where,
            device_id_type=MESH,
        )

    def first_sends(index):
        source = in_flight.at[0, pl.ds(index * rows, rows), :]
        return [
            (sector >= 1, remote(source, 0, index, 1, 0, (site, sector - 1))),
            (sector >= 3, remote(source, 0, index, 3, 1, (site, sector - 3))),
        ]

    def next_sends(tick, index):
        source = picked.at[tick, index]
        return [
            (has_next & (sector >= 1), remote(source, tick + 1, index, 1, 0, (site + 1, sector - 1))),
            (has_next & (sector >= 3), remote(source, tick + 1, index, 3, 1, (site + 1, sector - 3))),
            (has_next, remote(source, tick + 1, index, 0, 2, (site + 1, sector))),
        ]

    def entering_sends(tick, index):
        source = entering.at[tick, pl.ds(index * rows, rows), :]
        return [
            ((site == 0) & (sector >= 1), remote(source, tick + 1, index, 1, 3, (site, sector - 1))),
            ((site == 0) & (sector >= 3), remote(source, tick + 1, index, 3, 4, (site, sector - 3))),
        ]

    def by_left(of_sector):
        return (of_sector == 2) | ((site % 2 == 0) & (of_sector % side != 1))

    def relays(tick, index):
        one, three = sector + 1, sector + 3
        return [
            (
                (one <= last) & (sector >= 1) & by_left(one),
                remote(slots.at[tick, index, 1], tick, index, 2, 5, (site, sector - 1)),
            ),
            (
                (three <= last) & jnp.logical_not(by_left(three)),
                remote(slots.at[tick, index, 3], tick, index, 2, 6, (site, sector + 1)),
            ),
        ]

    def start(copies):
        for condition, copy in copies:
            when(condition)(copy.start)

    def finish(copies):
        for condition, copy in copies:
            when(condition)(copy.wait_send)

    def arrived(tick, index, count):
        remote(slots.at[tick, index, count], tick, index, count, 0, (site, sector)).wait_recv()

    def x_sends(tick, index, to_site):
        return [
            pltpu.make_async_remote_copy(
                src_ref=message.at[tick, index],
                dst_ref=along_x.at[tick + 1, index, x],
                send_sem=x_send_sem.at[tick, index],
                recv_sem=x_sem.at[tick + 1, index],
                device_id=(to_site, y * side + (x + hop) % side),
                device_id_type=MESH,
            )
            for hop in range(side)
        ]

    def y_sends(tick, index):
        return [
            pltpu.make_async_remote_copy(
                src_ref=along_y.at[tick, index, y],
                dst_ref=along_y.at[tick, index, y],
                send_sem=y_send_sem.at[tick, index],
                recv_sem=y_sem.at[tick, index],
                device_id=(site, (y + hop) % side * side + x),
                device_id_type=MESH,
            )
            for hop in range(1, side)
        ]

    def four(ref, tick, index):
        return (ref[tick, index, 0] + ref[tick, index, 1]) + (ref[tick, index, 2] + ref[tick, index, 3])

    def sums_to_rows(tick, index, parts):
        group = along_x.at[tick, index, pl.ds(0, parts)]
        pltpu.make_async_copy(group, group, x_sem.at[tick, index]).wait()
        along_y[tick, index, y] = four(along_x, tick, index)
        for copy in y_sends(tick, index):
            copy.start()

    def sums_arrived(tick, index):
        group = along_y.at[tick, index, pl.ds(0, side - 1)]
        pltpu.make_async_copy(group, group, y_sem.at[tick, index]).wait()

    def sums_of(tick, index):
        total = four(along_y, tick, index)
        picked_power = column_of(total, 0, rows) / bond + EPSILON
        total_power = column_of(total, rows, rows) / bond + EPSILON
        log_weight = column_of(total, 2 * rows, rows) / sectors
        scale = 1.0 / jnp.sqrt(picked_power)
        return scale, log_weight + jnp.log(picked_power) - jnp.log(total_power)

    def pass_on(tick, index):
        @when((tick > 0) & (site > 0))
        def _():
            sums_to_rows(tick, index, side)

        @when(sector + 1 <= last)
        def _():
            arrived(tick, index, 1)

        (left_condition, left), (right_condition, right) = relays(tick, index)
        when(left_condition)(left.start)

        @when(sector + 3 <= last)
        def _():
            arrived(tick, index, 3)

        when(right_condition)(right.start)

    def work(tick, index):
        is_first, is_entering = tick == 0, site == 0

        @when(is_first | is_entering)
        def _():
            pltpu.make_async_copy(slots.at[tick, index, 0], slots.at[tick, index, 0], slot_sem.at[tick, index, 0]).wait()

        @when(jnp.logical_not(is_first | is_entering))
        def _():
            arrived(tick, index, 0)
            sums_arrived(tick, index)

        @when(sector + 2 <= last)
        def _():
            arrived(tick, index, 2)

        products = []
        for count in range(4):
            block_high, block_low = halves(slots[tick, index, count])
            both = jnp.dot(
                jnp.concatenate([block_high, block_low], axis=0), high[count], preferred_element_type=jnp.float32
            )
            rest = jnp.dot(block_high, low[count], preferred_element_type=jnp.float32)
            products.append(both[:rows] + (both[rows:] + rest))
        scale, log_weight = sums_of(tick, index)
        fresh = is_first | is_entering
        scale = jnp.where(fresh, 1.0, scale)
        own_prior = jnp.where(is_first, column_of(prior[...], index * rows, rows), 0.0)
        log_weight = jnp.where(fresh, own_prior, log_weight)
        chosen = column_of(outcomes[tick].astype(jnp.float32), index * rows, rows)
        selected = jnp.zeros_like(products[0])
        squares = jnp.zeros_like(products[0])
        for count in range(4):
            amplitude = products[count] * scale
            selected = jnp.where(chosen == float(count), amplitude, selected)
            squares = squares + amplitude * amplitude
        picked[tick, index] = selected
        message[tick, index] = vector_of(
            [
                (0, jnp.sum(selected * selected, axis=1, keepdims=True)),
                (rows, jnp.sum(squares, axis=1, keepdims=True)),
                (2 * rows, log_weight),
            ],
            rows,
        )

        @when(tick < ticks - 1)
        def _():
            @when(has_next)
            def _():
                for copy in x_sends(tick, index, site + 1):
                    copy.start()

            start(next_sends(tick, index))
            start(entering_sends(tick, index))

        @when(tick == ticks - 1)
        def _():
            for copy in x_sends(tick, index, site)[1:]:
                copy.start()
            along_x[ticks, index, x] = message[tick, index]

    for index in range(CHUNKS):
        start(first_sends(index))

    @when(site == 0)
    def _():
        for tick in range(1, ticks):
            for index in range(CHUNKS):
                local_entering(tick, index).start()

    for count in range(4):
        raw_copies[count].wait()

        def cut(step, carry):
            part = pl.ds(pl.multiple_of(step * 64, 64), 64)
            high[count, part, :], low[count, part, :] = halves(raw[count, part, :])
            return carry

        lax.fori_loop(0, raw.shape[1] // 64, cut, 0)

    steps = ticks * CHUNKS
    pass_on(0, 0)

    def step(number, carry):
        @when(number + 1 < steps)
        def _():
            pass_on((number + 1) // CHUNKS, (number + 1) % CHUNKS)

        work(number // CHUNKS, number % CHUNKS)
        return carry

    lax.fori_loop(0, steps, step, 0)

    for index in range(CHUNKS):
        sums_to_rows(ticks, index, side - 1)
    final = jnp.zeros((1, LANES), jnp.float32)
    for index in range(CHUNKS):
        sums_arrived(ticks, index)
        scale, log_weight = sums_of(ticks, index)
        env_out[0, index * rows : (index + 1) * rows, :] = picked[ticks - 1, index] * scale
        final = final + vector_of([(index * rows, log_weight)], rows)
    logp_out[...] = final

    def drain(number, carry):
        tick, index = number // CHUNKS, number % CHUNKS
        finish(relays(tick, index))

        @when(tick < ticks - 1)
        def _():
            finish(next_sends(tick, index))
            finish(entering_sends(tick, index))

        parts = jnp.where(tick < ticks - 1, side, side - 1)

        @when((tick < ticks - 1) & has_next)
        def _():
            group = along_x.at[0, 0]
            pltpu.make_async_copy(group, group, x_send_sem.at[tick, index]).wait()

        @when(tick == ticks - 1)
        def _():
            group = along_x.at[0, 0, pl.ds(0, side - 1)]
            pltpu.make_async_copy(group, group, x_send_sem.at[tick, index]).wait()

        @when((tick > 0) & (site > 0))
        def _():
            group = along_y.at[0, 0, pl.ds(0, side - 1)]
            pltpu.make_async_copy(group, group, y_send_sem.at[tick, index]).wait()

        return carry

    lax.fori_loop(0, steps, drain, 0)
    for index in range(CHUNKS):
        finish(first_sends(index))
        group = along_y.at[0, 0, pl.ds(0, side - 1)]
        pltpu.make_async_copy(group, group, y_send_sem.at[ticks, index]).wait()


def solution(mesh):
    sites, sectors = mesh.shape["site"], mesh.shape["sector"]
    side = int(round(sectors**0.5))

    def per_device(site_tensor, outcomes, in_flight, prior_logp, entering):
        ticks = outcomes.shape[0]
        _, counts, _, width, _ = site_tensor.shape
        rows = in_flight.shape[1] // CHUNKS
        anywhere = pl.BlockSpec(memory_space=pl.ANY)
        vmem = pl.BlockSpec(memory_space=pltpu.VMEM)
        f32, dma = jnp.float32, pltpu.SemaphoreType.DMA
        return pl.pallas_call(
            functools.partial(kernel, ticks, side, sites, float(width * sectors)),
            name="chain",
            out_shape=(
                jax.ShapeDtypeStruct(in_flight.shape, f32),
                jax.ShapeDtypeStruct(prior_logp.shape, f32),
            ),
            in_specs=[anywhere, vmem, anywhere, vmem, anywhere],
            out_specs=(vmem, vmem),
            scratch_shapes=[
                pltpu.VMEM((counts, width, width), f32),
                pltpu.VMEM((counts, width, width), jnp.bfloat16),
                pltpu.VMEM((counts, width, width), jnp.bfloat16),
                pltpu.VMEM((ticks, CHUNKS, counts, rows, width), f32),
                pltpu.VMEM((ticks, CHUNKS, rows, width), f32),
                pltpu.VMEM((ticks, CHUNKS, 1, LANES), f32),
                pltpu.VMEM((ticks + 1, CHUNKS, side, 1, LANES), f32),
                pltpu.VMEM((ticks + 1, CHUNKS, side, 1, LANES), f32),
                dma((counts,)),
                dma((1,)),
                dma((ticks, CHUNKS, counts)),
                dma((ticks + 1, CHUNKS)),
                dma((ticks + 1, CHUNKS)),
                dma((7, ticks, CHUNKS)),
                dma((ticks, CHUNKS)),
                dma((ticks + 1, CHUNKS)),
            ],
            compiler_params=pltpu.CompilerParams(
                collective_id=0, has_side_effects=True, vmem_limit_bytes=48 * 1024 * 1024
            ),
            cost_estimate=pl.CostEstimate(
                flops=6 * ticks * counts * rows * CHUNKS * width * width,
                bytes_accessed=4 * counts * width * width,
                transcendentals=0,
            ),
        )(site_tensor, outcomes, in_flight, prior_logp, entering)

    return jax.shard_map(
        per_device,
        mesh=mesh,
        in_specs=(
            P("site", None, "sector", None, None),
            P(None, "site", None),
            P("site", None, "sector"),
            P("site", None),
            P(None, None, "sector"),
        ),
        out_specs=(P("site", None, "sector"), P("site", None)),
        check_vma=False,
    )
```

```python
import functools

import jax
import jax.numpy as jnp
from jax import lax
from jax.experimental import pallas as pl
from jax.experimental.pallas import tpu as pltpu
from jax.sharding import PartitionSpec as P

EPSILON = 1e-06
CHUNKS = 4
AHEAD = 2
LANES = 128
MESH = pl.DeviceIdType.MESH


def when(condition):
    return pl.when(condition)


def diagonal():
    lane = lax.broadcasted_iota(jnp.int32, (LANES, LANES), 1)
    row = lax.broadcasted_iota(jnp.int32, (LANES, LANES), 0)
    return lane == row


def column_of(vector):
    spread = jnp.where(diagonal(), jnp.broadcast_to(vector, (LANES, LANES)), 0.0)
    return jnp.broadcast_to(jnp.sum(spread, axis=1, keepdims=True), (LANES, LANES))


def sums_of_rows(value):
    spread = jnp.where(diagonal(), jnp.sum(value, axis=1, keepdims=True), 0.0)
    return jnp.sum(spread, axis=0, keepdims=True)


def halves(value):
    high = value.astype(jnp.bfloat16)
    return high, (value - high.astype(jnp.float32)).astype(jnp.bfloat16)


def kernel(
    ticks,
    side,
    sites,
    bond,
    site_tensor,
    outcomes_in,
    in_flight,
    prior_in,
    entering,
    env_out,
    logp_out,
    outcomes,
    prior,
    raw,
    high,
    low,
    slots,
    picked,
    chosen,
    scale,
    picked_fold,
    total_fold,
    carried,
    message,
    along_x,
    along_y,
    raw_sem,
    local_sem,
    slot_sem,
    x_sem,
    y_sem,
    send_sem,
    x_send_sem,
    y_send_sem,
):
    site, sector = lax.axis_index("site"), lax.axis_index("sector")
    x, y = sector % side, sector // side
    last = side * side - 1
    last_site = sites - 1
    next_site = (site + 1) % sites
    site_before = (site + sites - 1) % sites
    even = site % 2 == 0
    rows = slots.shape[3]
    width = slots.shape[4]
    tiles = width // LANES
    always = site >= 0

    raw_copies = [
        pltpu.make_async_copy(site_tensor.at[0, count, 0], raw.at[count], raw_sem.at[count]) for count in range(4)
    ]
    small_copies = [
        pltpu.make_async_copy(outcomes_in, outcomes, local_sem.at[0]),
        pltpu.make_async_copy(prior_in, prior, local_sem.at[1]),
    ]
    row_copies = [
        pltpu.make_async_copy(
            in_flight.at[0, pl.ds(index * rows, rows), :], slots.at[0, index, 0], slot_sem.at[0, index, 0]
        )
        for index in range(CHUNKS)
    ]

    def entering_copy(tick, index):
        return pltpu.make_async_copy(
            entering.at[tick, pl.ds(index * rows, rows), :], picked.at[tick, index], local_sem.at[2 + tick * CHUNKS + index]
        )

    barrier = pltpu.get_barrier_semaphore()
    expected = jnp.int32(0)

    def greet(from_condition, where, to_condition):
        @when(from_condition)
        def _():
            pl.semaphore_signal(barrier, inc=1, device_id=where, device_id_type=MESH)

        return to_condition.astype(jnp.int32)

    for near, own in ((site, False), (site_before, True)):
        for hop in range(0 if own else 1, side):
            expected += greet(always, (near, y * side + (x + hop) % side), always)
        for hop in range(1, side):
            expected += greet(always, (near, (y + hop) % side * side + x), always)
        expected += greet((x == side - 1) & (sector < last), (near, sector + 1), (x == 0) & (sector > 0))
        expected += greet((x != 0) & (sector + 3 <= last), (near, sector + 3), (x != side - 1) & (sector >= 3))
    expected += greet((x == 0) & (sector > 0), (site, sector - 1), (x == side - 1) & (sector < last))

    for copy in row_copies + small_copies + raw_copies:
        copy.start()

    pl.semaphore_wait(barrier, expected)

    def remote(source, tick, index, count, kind, where):
        return pltpu.make_async_remote_copy(
            src_ref=source,
            dst_ref=slots.at[tick, index, count],
            send_sem=send_sem.at[kind, tick, index],
            recv_sem=slot_sem.at[tick, index, count],
            device_id=where,
            device_id_type=MESH,
        )

    odd_to = next_site % 2 == 1

    def sends(source, tick, index, to_site, odd):
        first_column = odd & (x == 0)
        third_column = odd & (x == 2)
        return [
            ((sector >= 1) & jnp.logical_not(first_column), remote(source, tick, index, 1, 0, (to_site, sector - 1))),
            ((sector >= 3) & jnp.logical_not(third_column), remote(source, tick, index, 3, 1, (to_site, sector - 3))),
            ((sector >= side) & (first_column | third_column), remote(source, tick, index, 4, 2, (to_site, sector - side))),
            ((sector == 2) & jnp.logical_not(odd), remote(source, tick, index, 4, 2, (to_site, sector + 1))),
        ]

    def first_sends(index):
        return sends(in_flight.at[0, pl.ds(index * rows, rows), :], 0, index, site, jnp.logical_not(even))

    def next_sends(tick, index):
        source = picked.at[tick, index]
        own = (always, remote(source, tick + 1, index, 0, 3, (next_site, sector)))
        return sends(source, tick + 1, index, next_site, odd_to) + [own]

    def by_left(of_sector):
        return even == (of_sector % side < 2)

    left_on = (sector + 1 <= last) & (sector >= 1) & by_left(sector + 1)
    right_on = (sector + 3 <= last) & jnp.logical_not(by_left(sector + 3))
    crossed = jnp.logical_not(even) & (sector + side <= last)
    stage_first, stage_third = crossed & (x == 0), crossed & (x == 2)
    stage_two = even & (sector == 3)

    def relays(tick, index):
        stage, one, three = slots.at[tick, index, 4], slots.at[tick, index, 1], slots.at[tick, index, 3]
        return [
            (stage_first, 4, remote(stage, tick, index, 1, 4, (site, sector + 3))),
            (stage_third, 4, remote(stage, tick, index, 3, 4, (site, sector + 1))),
            (stage_two, 4, remote(stage, tick, index, 2, 4, (site, sector - 3))),
            (left_on, 1, remote(one, tick, index, 2, 5, (site, sector - 1))),
            (right_on, 3, remote(three, tick, index, 2, 6, (site, sector + 1))),
        ]

    def start(copies):
        for condition, copy in copies:
            when(condition)(copy.start)

    def finish(copies):
        for condition, copy in copies:
            when(condition)(copy.wait_send)

    def arrived(tick, index, count):
        remote(slots.at[tick, index, count], tick, index, count, 0, (site, sector)).wait_recv()

    def x_sends(tick, to_site):
        return [
            pltpu.make_async_remote_copy(
                src_ref=message.at[tick],
                dst_ref=along_x.at[tick + 1, x],
                send_sem=x_send_sem.at[tick],
                recv_sem=x_sem.at[tick + 1],
                device_id=(to_site, y * side + (x + hop) % side),
                device_id_type=MESH,
            )
            for hop in range(side)
        ]

    def y_sends(slot, to_site):
        return [
            pltpu.make_async_remote_copy(
                src_ref=carried.at[slot],
                dst_ref=along_y.at[slot, y],
                send_sem=y_send_sem.at[slot],
                recv_sem=y_sem.at[slot],
                device_id=(to_site, (y + hop) % side * side + x),
                device_id_type=MESH,
            )
            for hop in range(side)
        ]

    def wait_for(ref, sem):
        pltpu.make_async_copy(ref, ref, sem).wait()

    def four(ref, tick):
        return (ref[tick, 0] + ref[tick, 1]) + (ref[tick, 2] + ref[tick, 3])

    def advance(slot):
        sums = four(along_y, slot)
        before = along_y[slot, 0]
        before_log, before_scale = before[2:3], before[3:4]
        picked_power = sums[0:1] * before_scale * before_scale / bond + EPSILON
        total_power = sums[1:2] * before_scale * before_scale / bond + EPSILON
        return 1.0 / jnp.sqrt(picked_power), before_log + jnp.log(picked_power) - jnp.log(total_power)

    def age_at(tick):
        return jnp.minimum(tick, site)

    def begin(tick):
        age = age_at(tick)

        @when(age >= 2)
        def _():
            wait_for(along_y.at[tick], y_sem.at[tick])
            now_scale, now_log = advance(tick)
            carried[tick + 1, 2:3, :] = now_log
            carried[tick + 1, 3:4, :] = now_scale
            scale[...] = column_of(now_scale)

        @when(age < 2)
        def _():
            carried[tick + 1, 2:3, :] = jnp.where(tick == 0, prior[...], 0.0)
            carried[tick + 1, 3:4, :] = jnp.ones((1, LANES), jnp.float32)
            scale[...] = jnp.ones_like(scale)

    def middle(tick):
        @when(age_at(tick) >= 1)
        def _():
            wait_for(along_x.at[tick], x_sem.at[tick])
            sums = four(along_x, tick)
            carried[tick + 1, 0:2, :] = sums[0:2]

            @when(age_at(tick) == 1)
            def _():
                carried[tick + 1, 2:3, :] = along_x[tick, 0][2:3]

            @when((tick < ticks - 1) & (site < last_site))
            def _():
                for copy in y_sends(tick + 1, next_site):
                    copy.start()

            @when(tick == ticks - 1)
            def _():
                for copy in y_sends(ticks, site)[1:]:
                    copy.start()
                along_y[ticks, y] = carried[ticks]

    def end(tick):
        message[tick, 0:1, :] = sums_of_rows(picked_fold[...])
        message[tick, 1:2, :] = sums_of_rows(total_fold[...])
        message[tick, 2:3, :] = carried[tick + 1, 2:3, :]
        message[tick, 3:4, :] = carried[tick + 1, 3:4, :]

        @when((tick < ticks - 1) & (site < last_site))
        def _():
            for copy in x_sends(tick, next_site):
                copy.start()

        @when(tick == ticks - 1)
        def _():
            for copy in x_sends(tick, site)[1:]:
                copy.start()
            along_x[ticks, x] = message[ticks - 1]

    def pass_on(tick, index):
        for condition, count, copy in relays(tick, index):

            @when(condition)
            def _():
                arrived(tick, index, count)
                copy.start()

    def work(tick, index, meanwhile):
        @when(tick == 0)
        def _():
            wait_for(slots.at[0, index, 0], slot_sem.at[0, index, 0])

        @when(tick > 0)
        def _():
            arrived(tick, index, 0)

        part = pl.ds(pl.multiple_of(index * rows, rows), rows)
        factor = jnp.concatenate([scale[part, :]] * tiles, axis=1)
        choice = jnp.concatenate([chosen[tick, part, :]] * tiles, axis=1)
        selected = jnp.zeros((rows, width), jnp.float32)
        squares = jnp.zeros((rows, width), jnp.float32)
        for count in (0, 1, 3, 2):
            if count == 1:
                when((sector + 1 <= last) & jnp.logical_not(left_on))(lambda: arrived(tick, index, 1))
                when((sector + 3 <= last) & jnp.logical_not(right_on))(lambda: arrived(tick, index, 3))
            if count == 2:
                meanwhile()
                when(sector + 2 <= last)(lambda: arrived(tick, index, 2))
            block_high, block_low = halves(slots[tick, index, count])
            both = jnp.dot(
                jnp.concatenate([block_high, block_low], axis=0), high[count], preferred_element_type=jnp.float32
            )
            rest = jnp.dot(block_high, low[count], preferred_element_type=jnp.float32)
            amplitude = (both[:rows] + (both[rows:] + rest)) * factor
            selected = jnp.where(choice == float(count), amplitude, selected)
            squares = squares + amplitude * amplitude

        @when((site < last_site) | (tick == ticks - 1))
        def _():
            picked[tick, index] = selected

        @when(tick < ticks - 1)
        def _():
            start(next_sends(tick, index))

        def folded(value):
            return sum(value[:, tile * LANES : (tile + 1) * LANES] for tile in range(tiles))

        picked_fold[part, :] = folded(selected * selected)
        total_fold[part, :] = folded(squares)

    for index in range(CHUNKS):
        start(first_sends(index))

    @when(site == last_site)
    def _():
        for tick in range(ticks - 1):
            for index in range(CHUNKS):
                entering_copy(tick, index).start()

    for count in range(1, 4):

        @when(sector + count > last)
        def _():
            def clear(number, carry):
                slots[number // CHUNKS, number % CHUNKS, count] = jnp.zeros((rows, width), jnp.float32)
                return carry

            lax.fori_loop(0, ticks * CHUNKS, clear, 0)

    for count in range(4):
        raw_copies[count].wait()

        def cut(step, carry):
            part = pl.ds(pl.multiple_of(step * 64, 64), 64)
            high[count, part, :], low[count, part, :] = halves(raw[count, part, :])
            return carry

        lax.fori_loop(0, width // 64, cut, 0)

    @when(site == last_site)
    def _():
        for tick in range(ticks - 1):
            for index in range(CHUNKS):
                entering_copy(tick, index).wait()

    steps = ticks * CHUNKS
    pass_on(0, 0)

    for copy in small_copies:
        copy.wait()

    def choose(tick, carry):
        chosen[tick] = column_of(outcomes[tick].astype(jnp.float32))
        return carry

    lax.fori_loop(0, ticks, choose, 0)

    for number in range(1, AHEAD):
        pass_on(number // CHUNKS, number % CHUNKS)

    def step(number, carry):
        tick, index = number // CHUNKS, number % CHUNKS
        later = number + AHEAD

        @when(index == 0)
        def _():
            begin(tick)

        def meanwhile():
            @when(later < steps)
            def _():
                pass_on(later // CHUNKS, later % CHUNKS)

        work(tick, index, meanwhile)

        @when((index == CHUNKS // 2 - 1) & (tick > 0))
        def _():
            middle(tick)

        @when(index == CHUNKS - 1)
        def _():
            end(tick)

        return carry

    lax.fori_loop(0, steps, step, 0)

    @when(site >= 1)
    def _():
        wait_for(along_y.at[ticks, pl.ds(0, side - 1)], y_sem.at[ticks])
        now_scale, now_log = advance(ticks)
        carried[ticks + 1, 2:3, :] = now_log
        carried[ticks + 1, 3:4, :] = now_scale
        scale[...] = column_of(now_scale)

    @when(site == 0)
    def _():
        carried[ticks + 1, 2:3, :] = carried[ticks, 2:3, :]
        carried[ticks + 1, 3:4, :] = carried[ticks, 3:4, :]

    wait_for(along_x.at[ticks, pl.ds(0, side - 1)], x_sem.at[ticks])
    carried[ticks + 1, 0:2, :] = four(along_x, ticks)[0:2]
    for copy in y_sends(ticks + 1, site)[1:]:
        copy.start()
    along_y[ticks + 1, y] = carried[ticks + 1]

    for index in range(CHUNKS):
        finish(first_sends(index))

    def drain(number, carry):
        tick, index = number // CHUNKS, number % CHUNKS
        finish([(condition, copy) for condition, _, copy in relays(tick, index)])

        @when(tick < ticks - 1)
        def _():
            finish(next_sends(tick, index))

        return carry

    lax.fori_loop(0, steps, drain, 0)

    def drain_sums(tick, carry):
        @when(site < last_site)
        def _():
            wait_for(along_x.at[0], x_send_sem.at[tick])

        @when((age_at(tick) >= 1) & (site < last_site))
        def _():
            wait_for(along_y.at[0], y_send_sem.at[tick + 1])

        return carry

    lax.fori_loop(0, ticks - 1, drain_sums, 0)
    wait_for(along_x.at[0, pl.ds(0, side - 1)], x_send_sem.at[ticks - 1])

    @when(site >= 1)
    def _():
        wait_for(along_y.at[0, pl.ds(0, side - 1)], y_send_sem.at[ticks])

    wait_for(along_y.at[0, pl.ds(0, side - 1)], y_send_sem.at[ticks + 1])

    wait_for(along_y.at[ticks + 1, pl.ds(0, side - 1)], y_sem.at[ticks + 1])
    now_scale, now_log = advance(ticks + 1)
    logp_out[...] = now_log
    factor = scale[...] * column_of(now_scale)
    for index in range(CHUNKS):
        part = factor[index * rows : (index + 1) * rows]
        env_out[0, index * rows : (index + 1) * rows, :] = picked[ticks - 1, index] * jnp.concatenate([part] * tiles, axis=1)


def solution(mesh):
    sites, sectors = mesh.shape["site"], mesh.shape["sector"]
    side = int(round(sectors**0.5))

    def per_device(site_tensor, outcomes, in_flight, prior_logp, entering):
        ticks = outcomes.shape[0]
        _, counts, _, width, _ = site_tensor.shape
        rows = in_flight.shape[1] // CHUNKS
        vmem = pl.BlockSpec(memory_space=pltpu.VMEM)
        f32, dma = jnp.float32, pltpu.SemaphoreType.DMA
        return pl.pallas_call(
            functools.partial(kernel, ticks, side, sites, float(width * sectors)),
            name="chain",
            out_shape=(
                jax.ShapeDtypeStruct(in_flight.shape, f32),
                jax.ShapeDtypeStruct(prior_logp.shape, f32),
            ),
            in_specs=[pl.BlockSpec(memory_space=pltpu.HBM)] * 5,
            out_specs=(vmem, vmem),
            scratch_shapes=[
                pltpu.VMEM(outcomes.shape, jnp.int32),
                pltpu.VMEM(prior_logp.shape, f32),
                pltpu.VMEM((counts, width, width), f32),
                pltpu.VMEM((counts, width, width), jnp.bfloat16),
                pltpu.VMEM((counts, width, width), jnp.bfloat16),
                pltpu.VMEM((ticks, CHUNKS, counts + 1, rows, width), f32),
                pltpu.VMEM((ticks, CHUNKS, rows, width), f32),
                pltpu.VMEM((ticks, LANES, LANES), f32),
                pltpu.VMEM((LANES, LANES), f32),
                pltpu.VMEM((LANES, LANES), f32),
                pltpu.VMEM((LANES, LANES), f32),
                pltpu.VMEM((ticks + 2, 4, LANES), f32),
                pltpu.VMEM((ticks, 4, LANES), f32),
                pltpu.VMEM((ticks + 1, side, 4, LANES), f32),
                pltpu.VMEM((ticks + 2, side, 4, LANES), f32),
                dma((counts,)),
                dma((2 + ticks * CHUNKS,)),
                dma((ticks, CHUNKS, counts + 1)),
                dma((ticks + 1,)),
                dma((ticks + 2,)),
                dma((7, ticks, CHUNKS)),
                dma((ticks,)),
                dma((ticks + 2,)),
            ],
            compiler_params=pltpu.CompilerParams(
                collective_id=0, has_side_effects=True, vmem_limit_bytes=60 * 1024 * 1024
            ),
            cost_estimate=pl.CostEstimate(
                flops=6 * ticks * counts * rows * CHUNKS * width * width,
                bytes_accessed=4 * counts * width * width,
                transcendentals=0,
            ),
        )(site_tensor, outcomes, in_flight, prior_logp, entering)

    return jax.shard_map(
        per_device,
        mesh=mesh,
        in_specs=(
            P("site", None, "sector", None, None),
            P(None, "site", None),
            P("site", None, "sector"),
            P("site", None),
            P(None, None, "sector"),
        ),
        out_specs=(P("site", None, "sector"), P("site", None)),
        check_vma=False,
    )
```

```python
import functools

import jax
import jax.numpy as jnp
from jax import lax
from jax.experimental import pallas as pl
from jax.experimental.pallas import tpu as pltpu
from jax.sharding import PartitionSpec as P

EPSILON = 1e-06
CHUNKS = 4
AHEAD = 2
LANES = 128
MESH = pl.DeviceIdType.MESH


def when(condition):
    return pl.when(condition)


def diagonal():
    lane = lax.broadcasted_iota(jnp.int32, (LANES, LANES), 1)
    row = lax.broadcasted_iota(jnp.int32, (LANES, LANES), 0)
    return lane == row


def column_of(vector):
    spread = jnp.where(diagonal(), jnp.broadcast_to(vector, (LANES, LANES)), 0.0)
    return jnp.broadcast_to(jnp.sum(spread, axis=1, keepdims=True), (LANES, LANES))


def sums_of_rows(value):
    spread = jnp.where(diagonal(), jnp.sum(value, axis=1, keepdims=True), 0.0)
    return jnp.sum(spread, axis=0, keepdims=True)


def halves(value):
    high = value.astype(jnp.bfloat16)
    return high, (value - high.astype(jnp.float32)).astype(jnp.bfloat16)


def kernel(
    ticks,
    side,
    sites,
    bond,
    site_tensor,
    outcomes_in,
    in_flight,
    prior_in,
    entering,
    env_out,
    logp_out,
    outcomes,
    prior,
    raw,
    high,
    low,
    slots,
    picked,
    chosen,
    scale,
    picked_fold,
    total_fold,
    carried,
    message,
    along_x,
    along_y,
    along_all,
    raw_sem,
    local_sem,
    slot_sem,
    x_sem,
    y_sem,
    all_sem,
    send_sem,
    x_send_sem,
    y_send_sem,
    all_send_sem,
):
    site, sector = lax.axis_index("site"), lax.axis_index("sector")
    x, y = sector % side, sector // side
    last = side * side - 1
    last_site = sites - 1
    next_site = (site + 1) % sites
    site_before = (site + sites - 1) % sites
    even = site % 2 == 0
    rows = slots.shape[3]
    width = slots.shape[4]
    tiles = width // LANES
    always = site >= 0

    raw_copies = [
        pltpu.make_async_copy(site_tensor.at[0, count, 0], raw.at[count], raw_sem.at[count]) for count in range(4)
    ]
    small_copies = [
        pltpu.make_async_copy(outcomes_in, outcomes, local_sem.at[0]),
        pltpu.make_async_copy(prior_in, prior, local_sem.at[1]),
    ]
    row_copies = [
        pltpu.make_async_copy(
            in_flight.at[0, pl.ds(index * rows, rows), :], slots.at[0, index, 0], slot_sem.at[0, index, 0]
        )
        for index in range(CHUNKS)
    ]

    def entering_copy(tick, index):
        return pltpu.make_async_copy(
            entering.at[tick, pl.ds(index * rows, rows), :], picked.at[tick, index], local_sem.at[2 + tick * CHUNKS + index]
        )

    barrier = pltpu.get_barrier_semaphore()
    expected = jnp.int32(0)

    def greet(from_condition, where, to_condition):
        @when(from_condition)
        def _():
            pl.semaphore_signal(barrier, inc=1, device_id=where, device_id_type=MESH)

        return to_condition.astype(jnp.int32)

    for hop in range(side):
        expected += greet(always, (site_before, y * side + (x + hop) % side), always)
    for hop in range(1, side):
        expected += greet(always, (site_before, (y + hop) % side * side + x), always)
    expected += greet((x == side - 1) & (sector < last), (site_before, sector + 1), (x == 0) & (sector > 0))
    expected += greet((x != 0) & (sector + 3 <= last), (site_before, sector + 3), (x != side - 1) & (sector >= 3))
    expected += greet(sector == last, (site_before, 0 * sector + 2), sector == 2)
    for hop in range(1, last + 1):
        expected += greet(always, (site, (sector + hop) % (last + 1)), always)

    for copy in row_copies + small_copies + raw_copies:
        copy.start()

    pl.semaphore_wait(barrier, expected)

    def remote(source, tick, index, count, kind, where):
        return pltpu.make_async_remote_copy(
            src_ref=source,
            dst_ref=slots.at[tick, index, count],
            send_sem=send_sem.at[kind, tick, index],
            recv_sem=slot_sem.at[tick, index, count],
            device_id=where,
            device_id_type=MESH,
        )

    odd_to = next_site % 2 == 1

    def sends(source, tick, index, to_site, odd):
        first_column = odd & (x == 0)
        third_column = odd & (x == 2)
        to_left = (sector >= 1) & jnp.logical_not(first_column)
        left = remote(source, tick, index, 1, 0, (to_site, sector - 1))
        left_first = odd == (x >= 2)
        return [
            (to_left & left_first, left),
            ((sector >= 3) & jnp.logical_not(third_column), remote(source, tick, index, 3, 1, (to_site, sector - 3))),
            ((sector >= side) & (first_column | third_column), remote(source, tick, index, 4, 2, (to_site, sector - side))),
            ((sector == 2) & jnp.logical_not(odd), remote(source, tick, index, 4, 2, (to_site, last))),
            (to_left & jnp.logical_not(left_first), left),
        ]

    def first_sends(index):
        return sends(in_flight.at[0, pl.ds(index * rows, rows), :], 0, index, site, jnp.logical_not(even))

    def next_sends(tick, index):
        source = picked.at[tick, index]
        own = (always, remote(source, tick + 1, index, 0, 3, (next_site, sector)))
        return sends(source, tick + 1, index, next_site, odd_to) + [own]

    def by_left(of_sector):
        return even == (of_sector % side < 2)

    left_on = (sector + 1 <= last) & (sector >= 1) & by_left(sector + 1)
    right_on = (sector + 3 <= last) & jnp.logical_not(by_left(sector + 3))
    crossed = jnp.logical_not(even) & (sector + side <= last)
    stage_first, stage_third = crossed & (x == 0), crossed & (x == 2)
    stage_two = even & (sector == last)

    def relays(tick, index):
        stage, one, three = slots.at[tick, index, 4], slots.at[tick, index, 1], slots.at[tick, index, 3]
        return [
            (stage_first, 4, remote(stage, tick, index, 1, 4, (site, sector + 3))),
            (stage_third, 4, remote(stage, tick, index, 3, 4, (site, sector + 1))),
            (stage_two, 4, remote(stage, tick, index, 2, 4, (site, 0 * sector))),
            (left_on, 1, remote(one, tick, index, 2, 5, (site, sector - 1))),
            (right_on, 3, remote(three, tick, index, 2, 6, (site, sector + 1))),
        ]

    def start(copies):
        for condition, copy in copies:
            when(condition)(copy.start)

    def finish(copies):
        for condition, copy in copies:
            when(condition)(copy.wait_send)

    def arrived(tick, index, count):
        remote(slots.at[tick, index, count], tick, index, count, 0, (site, sector)).wait_recv()

    def x_sends(tick, to_site):
        return [
            pltpu.make_async_remote_copy(
                src_ref=message.at[tick],
                dst_ref=along_x.at[tick + 1, x],
                send_sem=x_send_sem.at[tick],
                recv_sem=x_sem.at[tick + 1],
                device_id=(to_site, y * side + (x + hop) % side),
                device_id_type=MESH,
            )
            for hop in range(side)
        ]

    def y_sends(slot, to_site):
        return [
            pltpu.make_async_remote_copy(
                src_ref=carried.at[slot],
                dst_ref=along_y.at[slot, y],
                send_sem=y_send_sem.at[slot],
                recv_sem=y_sem.at[slot],
                device_id=(to_site, (y + hop) % side * side + x),
                device_id_type=MESH,
            )
            for hop in range(side)
        ]

    def all_sends():
        return [
            pltpu.make_async_remote_copy(
                src_ref=message.at[ticks - 1],
                dst_ref=along_all.at[sector],
                send_sem=all_send_sem.at[0],
                recv_sem=all_sem.at[0],
                device_id=(site, (sector + hop) % (last + 1)),
                device_id_type=MESH,
            )
            for hop in range(1, last + 1)
        ]

    def wait_for(ref, sem):
        pltpu.make_async_copy(ref, ref, sem).wait()

    def four(ref, tick):
        return (ref[tick, 0] + ref[tick, 1]) + (ref[tick, 2] + ref[tick, 3])

    def advance(sums, before_log, before_scale):
        picked_power = sums[0:1] * before_scale * before_scale / bond + EPSILON
        total_power = sums[1:2] * before_scale * before_scale / bond + EPSILON
        return 1.0 / jnp.sqrt(picked_power), before_log + jnp.log(picked_power) - jnp.log(total_power)

    def advance_from(slot):
        before = along_y[slot, 0]
        return advance(four(along_y, slot), before[2:3], before[3:4])

    def age_at(tick):
        return jnp.minimum(tick, site)

    def begin(tick):
        age = age_at(tick)

        @when(age >= 2)
        def _():
            wait_for(along_y.at[tick], y_sem.at[tick])
            now_scale, now_log = advance_from(tick)
            carried[tick + 1, 2:3, :] = now_log
            carried[tick + 1, 3:4, :] = now_scale
            scale[...] = column_of(now_scale)

        @when(age < 2)
        def _():
            carried[tick + 1, 2:3, :] = jnp.where(tick == 0, prior[...], 0.0)
            carried[tick + 1, 3:4, :] = jnp.ones((1, LANES), jnp.float32)
            scale[...] = jnp.ones_like(scale)

    def middle(tick):
        @when(age_at(tick) >= 1)
        def _():
            wait_for(along_x.at[tick], x_sem.at[tick])
            sums = four(along_x, tick)
            carried[tick + 1, 0:2, :] = sums[0:2]

            @when(age_at(tick) == 1)
            def _():
                carried[tick + 1, 2:3, :] = along_x[tick, 0][2:3]

            @when((tick < ticks - 1) & (site < last_site))
            def _():
                for copy in y_sends(tick + 1, next_site):
                    copy.start()

            @when(tick == ticks - 1)
            def _():
                for copy in y_sends(ticks, site)[1:]:
                    copy.start()
                along_y[ticks, y] = carried[ticks]

    def end(tick):
        message[tick, 0:1, :] = sums_of_rows(picked_fold[...])
        message[tick, 1:2, :] = sums_of_rows(total_fold[...])
        message[tick, 2:3, :] = carried[tick + 1, 2:3, :]
        message[tick, 3:4, :] = carried[tick + 1, 3:4, :]

        @when((tick < ticks - 1) & (site < last_site))
        def _():
            for copy in x_sends(tick, next_site):
                copy.start()

        @when(tick == ticks - 1)
        def _():
            for copy in all_sends():
                copy.start()
            along_all[sector] = message[ticks - 1]

    def pass_on(tick, index):
        for condition, count, copy in relays(tick, index):

            @when(condition)
            def _():
                arrived(tick, index, count)
                copy.start()

    def work(tick, index, meanwhile):
        @when(tick == 0)
        def _():
            wait_for(slots.at[0, index, 0], slot_sem.at[0, index, 0])

        @when(tick > 0)
        def _():
            arrived(tick, index, 0)

        part = pl.ds(pl.multiple_of(index * rows, rows), rows)
        factor = jnp.concatenate([scale[part, :]] * tiles, axis=1)
        choice = jnp.concatenate([chosen[tick, part, :]] * tiles, axis=1)
        selected = jnp.zeros((rows, width), jnp.float32)
        squares = jnp.zeros((rows, width), jnp.float32)
        for count in (0, 1, 3, 2):
            if count == 1:
                when((sector + 1 <= last) & jnp.logical_not(left_on))(lambda: arrived(tick, index, 1))
                when((sector + 3 <= last) & jnp.logical_not(right_on))(lambda: arrived(tick, index, 3))
            if count == 2:
                meanwhile()
                when(sector + 2 <= last)(lambda: arrived(tick, index, 2))
            block_high, block_low = halves(slots[tick, index, count])
            both = jnp.dot(
                jnp.concatenate([block_high, block_low], axis=0), high[count], preferred_element_type=jnp.float32
            )
            rest = jnp.dot(block_high, low[count], preferred_element_type=jnp.float32)
            amplitude = (both[:rows] + (both[rows:] + rest)) * factor
            selected = jnp.where(choice == float(count), amplitude, selected)
            squares = squares + amplitude * amplitude

        @when((site < last_site) | (tick == ticks - 1))
        def _():
            picked[tick, index] = selected

        @when(tick < ticks - 1)
        def _():
            start(next_sends(tick, index))

        def folded(value):
            return sum(value[:, tile * LANES : (tile + 1) * LANES] for tile in range(tiles))

        picked_fold[part, :] = folded(selected * selected)
        total_fold[part, :] = folded(squares)

    for index in range(CHUNKS):
        start(first_sends(index))

    @when(site == last_site)
    def _():
        for tick in range(ticks - 1):
            for index in range(CHUNKS):
                entering_copy(tick, index).start()

    for count in range(1, 4):

        @when(sector + count > last)
        def _():
            def clear(number, carry):
                slots[number // CHUNKS, number % CHUNKS, count] = jnp.zeros((rows, width), jnp.float32)
                return carry

            lax.fori_loop(0, ticks * CHUNKS, clear, 0)

    for count in range(4):
        raw_copies[count].wait()

        def cut(step, carry):
            part = pl.ds(pl.multiple_of(step * 64, 64), 64)
            high[count, part, :], low[count, part, :] = halves(raw[count, part, :])
            return carry

        lax.fori_loop(0, width // 64, cut, 0)

    @when(site == last_site)
    def _():
        for tick in range(ticks - 1):
            for index in range(CHUNKS):
                entering_copy(tick, index).wait()

    steps = ticks * CHUNKS
    pass_on(0, 0)

    for copy in small_copies:
        copy.wait()

    def choose(tick, carry):
        chosen[tick] = column_of(outcomes[tick].astype(jnp.float32))
        return carry

    lax.fori_loop(0, ticks, choose, 0)

    for number in range(1, AHEAD):
        pass_on(number // CHUNKS, number % CHUNKS)

    def step(number, carry):
        tick, index = number // CHUNKS, number % CHUNKS
        later = number + AHEAD

        @when(index == 0)
        def _():
            begin(tick)

        def meanwhile():
            @when(later < steps)
            def _():
                pass_on(later // CHUNKS, later % CHUNKS)

        work(tick, index, meanwhile)

        @when((index == CHUNKS // 2 - 1) & (tick > 0))
        def _():
            middle(tick)

        @when(index == CHUNKS - 1)
        def _():
            end(tick)

        return carry

    lax.fori_loop(0, steps, step, 0)

    @when(site >= 1)
    def _():
        wait_for(along_y.at[ticks, pl.ds(0, side - 1)], y_sem.at[ticks])
        now_scale, now_log = advance_from(ticks)
        carried[ticks + 1, 2:3, :] = now_log
        carried[ticks + 1, 3:4, :] = now_scale
        scale[...] = column_of(now_scale)

    @when(site == 0)
    def _():
        carried[ticks + 1, 2:3, :] = carried[ticks, 2:3, :]
        carried[ticks + 1, 3:4, :] = carried[ticks, 3:4, :]

    for index in range(CHUNKS):
        finish(first_sends(index))

    def drain(number, carry):
        tick, index = number // CHUNKS, number % CHUNKS
        finish([(condition, copy) for condition, _, copy in relays(tick, index)])

        @when(tick < ticks - 1)
        def _():
            finish(next_sends(tick, index))

        return carry

    lax.fori_loop(0, steps, drain, 0)

    def drain_sums(tick, carry):
        @when(site < last_site)
        def _():
            wait_for(along_x.at[0], x_send_sem.at[tick])

        @when((age_at(tick) >= 1) & (site < last_site))
        def _():
            wait_for(along_y.at[0], y_send_sem.at[tick + 1])

        return carry

    lax.fori_loop(0, ticks - 1, drain_sums, 0)
    @when(site >= 1)
    def _():
        wait_for(along_y.at[0, pl.ds(0, side - 1)], y_send_sem.at[ticks])

    all_but_one = along_all.at[pl.ds(0, last)]
    wait_for(all_but_one, all_send_sem.at[0])
    wait_for(all_but_one, all_sem.at[0])
    last_sums = [along_all[of_sector] for of_sector in range(side * side)]
    while len(last_sums) > 1:
        last_sums = [one + other for one, other in zip(last_sums[::2], last_sums[1::2])]
    last_sums = last_sums[0]
    now_scale, now_log = advance(last_sums, carried[ticks + 1, 2:3, :], carried[ticks + 1, 3:4, :])
    logp_out[...] = now_log
    factor = scale[...] * column_of(now_scale)
    for index in range(CHUNKS):
        part = factor[index * rows : (index + 1) * rows]
        env_out[0, index * rows : (index + 1) * rows, :] = picked[ticks - 1, index] * jnp.concatenate([part] * tiles, axis=1)


def solution(mesh):
    sites, sectors = mesh.shape["site"], mesh.shape["sector"]
    side = int(round(sectors**0.5))

    def per_device(site_tensor, outcomes, in_flight, prior_logp, entering):
        ticks = outcomes.shape[0]
        _, counts, _, width, _ = site_tensor.shape
        rows = in_flight.shape[1] // CHUNKS
        vmem = pl.BlockSpec(memory_space=pltpu.VMEM)
        f32, dma = jnp.float32, pltpu.SemaphoreType.DMA
        return pl.pallas_call(
            functools.partial(kernel, ticks, side, sites, float(width * sectors)),
            name="chain",
            out_shape=(
                jax.ShapeDtypeStruct(in_flight.shape, f32),
                jax.ShapeDtypeStruct(prior_logp.shape, f32),
            ),
            in_specs=[pl.BlockSpec(memory_space=pltpu.HBM)] * 5,
            out_specs=(vmem, vmem),
            scratch_shapes=[
                pltpu.VMEM(outcomes.shape, jnp.int32),
                pltpu.VMEM(prior_logp.shape, f32),
                pltpu.VMEM((counts, width, width), f32),
                pltpu.VMEM((counts, width, width), jnp.bfloat16),
                pltpu.VMEM((counts, width, width), jnp.bfloat16),
                pltpu.VMEM((ticks, CHUNKS, counts + 1, rows, width), f32),
                pltpu.VMEM((ticks, CHUNKS, rows, width), f32),
                pltpu.VMEM((ticks, LANES, LANES), f32),
                pltpu.VMEM((LANES, LANES), f32),
                pltpu.VMEM((LANES, LANES), f32),
                pltpu.VMEM((LANES, LANES), f32),
                pltpu.VMEM((ticks + 2, 4, LANES), f32),
                pltpu.VMEM((ticks, 4, LANES), f32),
                pltpu.VMEM((ticks, side, 4, LANES), f32),
                pltpu.VMEM((ticks + 1, side, 4, LANES), f32),
                pltpu.VMEM((side * side, 4, LANES), f32),
                dma((counts,)),
                dma((2 + ticks * CHUNKS,)),
                dma((ticks, CHUNKS, counts + 1)),
                dma((ticks,)),
                dma((ticks + 1,)),
                dma((1,)),
                dma((7, ticks, CHUNKS)),
                dma((ticks,)),
                dma((ticks + 1,)),
                dma((1,)),
            ],
            compiler_params=pltpu.CompilerParams(
                collective_id=0, has_side_effects=True, vmem_limit_bytes=48 * 1024 * 1024
            ),
            cost_estimate=pl.CostEstimate(
                flops=6 * ticks * counts * rows * CHUNKS * width * width,
                bytes_accessed=4 * counts * width * width,
                transcendentals=0,
            ),
        )(
            *(
                pltpu.with_memory_space_constraint(array, pltpu.HBM)
                for array in (site_tensor, outcomes, in_flight, prior_logp, entering)
            )
        )

    return jax.shard_map(
        per_device,
        mesh=mesh,
        in_specs=(
            P("site", None, "sector", None, None),
            P(None, "site", None),
            P("site", None, "sector"),
            P("site", None),
            P(None, None, "sector"),
        ),
        out_specs=(P("site", None, "sector"), P("site", None)),
        check_vma=False,
    )
```

```python
import functools

import jax
import jax.numpy as jnp
from jax import lax
from jax.experimental import pallas as pl
from jax.experimental.pallas import tpu as pltpu
from jax.sharding import PartitionSpec as P

EPSILON = 1e-06
CHUNKS = 4
AHEAD = 2
LANES = 128
MESH = pl.DeviceIdType.MESH


def when(condition):
    return pl.when(condition)


def diagonal():
    lane = lax.broadcasted_iota(jnp.int32, (LANES, LANES), 1)
    row = lax.broadcasted_iota(jnp.int32, (LANES, LANES), 0)
    return lane == row


def column_of(vector):
    spread = jnp.where(diagonal(), jnp.broadcast_to(vector, (LANES, LANES)), 0.0)
    return jnp.broadcast_to(jnp.sum(spread, axis=1, keepdims=True), (LANES, LANES))


def sums_of_rows(value):
    spread = jnp.where(diagonal(), jnp.sum(value, axis=1, keepdims=True), 0.0)
    return jnp.sum(spread, axis=0, keepdims=True)


def halves(value):
    high = value.astype(jnp.bfloat16)
    return high, (value - high.astype(jnp.float32)).astype(jnp.bfloat16)


def kernel(
    ticks,
    side,
    sites,
    bond,
    site_tensor,
    outcomes_in,
    in_flight,
    prior_in,
    entering,
    env_out,
    logp_out,
    outcomes,
    prior,
    raw,
    high,
    low,
    slots,
    picked,
    chosen,
    scale,
    picked_fold,
    total_fold,
    carried,
    message,
    along_x,
    along_y,
    along_all,
    raw_sem,
    local_sem,
    slot_sem,
    x_sem,
    y_sem,
    all_sem,
    send_sem,
    x_send_sem,
    y_send_sem,
    all_send_sem,
):
    site, sector = lax.axis_index("site"), lax.axis_index("sector")
    x, y = sector % side, sector // side
    last = side * side - 1
    last_site = sites - 1
    next_site = (site + 1) % sites
    site_before = (site + sites - 1) % sites
    even = site % 2 == 0
    rows = slots.shape[3]
    width = slots.shape[4]
    tiles = width // LANES
    always = site >= 0

    raw_copies = [
        pltpu.make_async_copy(site_tensor.at[0, count, 0], raw.at[count], raw_sem.at[count]) for count in range(4)
    ]
    small_copies = [
        pltpu.make_async_copy(outcomes_in, outcomes, local_sem.at[0]),
        pltpu.make_async_copy(prior_in, prior, local_sem.at[1]),
    ]
    row_copies = [
        pltpu.make_async_copy(
            in_flight.at[0, pl.ds(index * rows, rows), :], slots.at[0, index, 0], slot_sem.at[0, index, 0]
        )
        for index in range(CHUNKS)
    ]

    def entering_copy(tick, index):
        return pltpu.make_async_copy(
            entering.at[tick, pl.ds(index * rows, rows), :], picked.at[tick, index], local_sem.at[2 + tick * CHUNKS + index]
        )

    barrier = pltpu.get_barrier_semaphore()
    expected = jnp.int32(0)

    def greet(from_condition, where, to_condition):
        @when(from_condition)
        def _():
            pl.semaphore_signal(barrier, inc=1, device_id=where, device_id_type=MESH)

        return to_condition.astype(jnp.int32)

    for hop in range(side):
        expected += greet(always, (site_before, y * side + (x + hop) % side), always)
    for hop in range(1, side):
        expected += greet(always, (site_before, (y + hop) % side * side + x), always)
    expected += greet((x == side - 1) & (sector < last), (site_before, sector + 1), (x == 0) & (sector > 0))
    expected += greet((x != 0) & (sector + 3 <= last), (site_before, sector + 3), (x != side - 1) & (sector >= 3))
    expected += greet(sector == last, (site_before, 0 * sector + 2), sector == 2)
    for hop in range(1, last + 1):
        expected += greet(always, (site, (sector + hop) % (last + 1)), always)

    for copy in row_copies + small_copies + raw_copies:
        copy.start()

    for count in range(4):
        raw_copies[count].wait()

        def cut(step, carry):
            part = pl.ds(pl.multiple_of(step * 64, 64), 64)
            high[count, part, :], low[count, part, :] = halves(raw[count, part, :])
            return carry

        lax.fori_loop(0, width // 64, cut, 0)

    pl.semaphore_wait(barrier, expected)

    def remote(source, tick, index, count, kind, where):
        return pltpu.make_async_remote_copy(
            src_ref=source,
            dst_ref=slots.at[tick, index, count],
            send_sem=send_sem.at[kind, tick, index],
            recv_sem=slot_sem.at[tick, index, count],
            device_id=where,
            device_id_type=MESH,
        )

    odd_to = next_site % 2 == 1

    def sends(source, tick, index, to_site, odd):
        first_column = odd & (x == 0)
        third_column = odd & (x == 2)
        to_left = (sector >= 1) & jnp.logical_not(first_column)
        left = remote(source, tick, index, 1, 0, (to_site, sector - 1))
        left_first = odd == (x >= 2)
        return [
            (to_left & left_first, left),
            ((sector >= 3) & jnp.logical_not(third_column), remote(source, tick, index, 3, 1, (to_site, sector - 3))),
            ((sector >= side) & (first_column | third_column), remote(source, tick, index, 4, 2, (to_site, sector - side))),
            ((sector == 2) & jnp.logical_not(odd), remote(source, tick, index, 4, 2, (to_site, last))),
            (to_left & jnp.logical_not(left_first), left),
        ]

    def first_sends(index):
        return sends(in_flight.at[0, pl.ds(index * rows, rows), :], 0, index, site, jnp.logical_not(even))

    def next_sends(tick, index):
        source = picked.at[tick, index]
        own = (always, remote(source, tick + 1, index, 0, 3, (next_site, sector)))
        return sends(source, tick + 1, index, next_site, odd_to) + [own]

    def by_left(of_sector):
        return even == (of_sector % side < 2)

    left_on = (sector + 1 <= last) & (sector >= 1) & by_left(sector + 1)
    right_on = (sector + 3 <= last) & jnp.logical_not(by_left(sector + 3))
    crossed = jnp.logical_not(even) & (sector + side <= last)
    stage_first, stage_third = crossed & (x == 0), crossed & (x == 2)
    stage_two = even & (sector == last)

    def relays(tick, index):
        stage, one, three = slots.at[tick, index, 4], slots.at[tick, index, 1], slots.at[tick, index, 3]
        return [
            (stage_first, 4, remote(stage, tick, index, 1, 4, (site, sector + 3))),
            (stage_third, 4, remote(stage, tick, index, 3, 4, (site, sector + 1))),
            (stage_two, 4, remote(stage, tick, index, 2, 4, (site, 0 * sector))),
            (left_on, 1, remote(one, tick, index, 2, 5, (site, sector - 1))),
            (right_on, 3, remote(three, tick, index, 2, 6, (site, sector + 1))),
        ]

    def start(copies):
        for condition, copy in copies:
            when(condition)(copy.start)

    def finish(copies):
        for condition, copy in copies:
            when(condition)(copy.wait_send)

    def arrived(tick, index, count):
        remote(slots.at[tick, index, count], tick, index, count, 0, (site, sector)).wait_recv()

    def x_sends(tick, to_site):
        return [
            pltpu.make_async_remote_copy(
                src_ref=message.at[tick],
                dst_ref=along_x.at[tick + 1, x],
                send_sem=x_send_sem.at[tick],
                recv_sem=x_sem.at[tick + 1],
                device_id=(to_site, y * side + (x + hop) % side),
                device_id_type=MESH,
            )
            for hop in range(side)
        ]

    def y_sends(slot, to_site):
        return [
            pltpu.make_async_remote_copy(
                src_ref=carried.at[slot],
                dst_ref=along_y.at[slot, y],
                send_sem=y_send_sem.at[slot],
                recv_sem=y_sem.at[slot],
                device_id=(to_site, (y + hop) % side * side + x),
                device_id_type=MESH,
            )
            for hop in range(side)
        ]

    def all_sends():
        return [
            pltpu.make_async_remote_copy(
                src_ref=message.at[ticks - 1],
                dst_ref=along_all.at[sector],
                send_sem=all_send_sem.at[0],
                recv_sem=all_sem.at[0],
                device_id=(site, (sector + hop) % (last + 1)),
                device_id_type=MESH,
            )
            for hop in range(1, last + 1)
        ]

    def wait_for(ref, sem):
        pltpu.make_async_copy(ref, ref, sem).wait()

    def four(ref, tick):
        return (ref[tick, 0] + ref[tick, 1]) + (ref[tick, 2] + ref[tick, 3])

    def advance(sums, before_log, before_scale):
        picked_power = sums[0:1] * before_scale * before_scale / bond + EPSILON
        total_power = sums[1:2] * before_scale * before_scale / bond + EPSILON
        return 1.0 / jnp.sqrt(picked_power), before_log + jnp.log(picked_power) - jnp.log(total_power)

    def advance_from(slot):
        before = along_y[slot, 0]
        return advance(four(along_y, slot), before[2:3], before[3:4])

    def age_at(tick):
        return jnp.minimum(tick, site)

    def begin(tick):
        age = age_at(tick)
        chosen[...] = column_of(outcomes[tick].astype(jnp.float32))

        @when(age >= 2)
        def _():
            wait_for(along_y.at[tick], y_sem.at[tick])
            now_scale, now_log = advance_from(tick)
            carried[tick + 1, 2:3, :] = now_log
            carried[tick + 1, 3:4, :] = now_scale
            scale[...] = column_of(now_scale)

        @when(age < 2)
        def _():
            carried[tick + 1, 2:3, :] = jnp.where(tick == 0, prior[...], 0.0)
            carried[tick + 1, 3:4, :] = jnp.ones((1, LANES), jnp.float32)
            scale[...] = jnp.ones((LANES, LANES), jnp.float32)

    def middle(tick):
        @when(age_at(tick) >= 1)
        def _():
            wait_for(along_x.at[tick], x_sem.at[tick])
            sums = four(along_x, tick)
            carried[tick + 1, 0:2, :] = sums[0:2]

            @when(age_at(tick) == 1)
            def _():
                carried[tick + 1, 2:3, :] = along_x[tick, 0][2:3]

            @when((tick < ticks - 1) & (site < last_site))
            def _():
                for copy in y_sends(tick + 1, next_site):
                    copy.start()

            @when(tick == ticks - 1)
            def _():
                for copy in y_sends(ticks, site)[1:]:
                    copy.start()
                along_y[ticks, y] = carried[ticks]

    def end(tick):
        message[tick, 0:1, :] = sums_of_rows(picked_fold[...])
        message[tick, 1:2, :] = sums_of_rows(total_fold[...])
        message[tick, 2:3, :] = carried[tick + 1, 2:3, :]
        message[tick, 3:4, :] = carried[tick + 1, 3:4, :]

        @when((tick < ticks - 1) & (site < last_site))
        def _():
            for copy in x_sends(tick, next_site):
                copy.start()

        @when(tick == ticks - 1)
        def _():
            for copy in all_sends():
                copy.start()
            along_all[sector] = message[ticks - 1]

    def pass_on(tick, index):
        for condition, count, copy in relays(tick, index):

            @when(condition)
            def _():
                arrived(tick, index, count)
                copy.start()

    def work(tick, index, meanwhile):
        @when(tick == 0)
        def _():
            wait_for(slots.at[0, index, 0], slot_sem.at[0, index, 0])

        @when(tick > 0)
        def _():
            arrived(tick, index, 0)

        part = pl.ds(pl.multiple_of(index * rows, rows), rows)
        factor = jnp.concatenate([scale[part, :]] * tiles, axis=1)
        choice = jnp.concatenate([chosen[part, :]] * tiles, axis=1)
        selected = jnp.zeros((rows, width), jnp.float32)
        squares = jnp.zeros((rows, width), jnp.float32)
        for count in (0, 1, 3, 2):
            if count == 1:
                when((sector + 1 <= last) & jnp.logical_not(left_on))(lambda: arrived(tick, index, 1))
                when((sector + 3 <= last) & jnp.logical_not(right_on))(lambda: arrived(tick, index, 3))
            if count == 2:
                meanwhile()
                when(sector + 2 <= last)(lambda: arrived(tick, index, 2))
            block_high, block_low = halves(slots[tick, index, count])
            both = jnp.dot(
                jnp.concatenate([block_high, block_low], axis=0), high[count], preferred_element_type=jnp.float32
            )
            rest = jnp.dot(block_high, low[count], preferred_element_type=jnp.float32)
            amplitude = (both[:rows] + (both[rows:] + rest)) * factor
            selected = jnp.where(choice == float(count), amplitude, selected)
            squares = squares + amplitude * amplitude

        @when((site < last_site) | (tick == ticks - 1))
        def _():
            picked[tick, index] = selected

        @when(tick < ticks - 1)
        def _():
            start(next_sends(tick, index))

        def folded(value):
            return sum(value[:, tile * LANES : (tile + 1) * LANES] for tile in range(tiles))

        picked_fold[part, :] = folded(selected * selected)
        total_fold[part, :] = folded(squares)

    for index in range(AHEAD):
        start(first_sends(index))

    @when(site == last_site)
    def _():
        for tick in range(ticks - 1):
            for index in range(CHUNKS):
                entering_copy(tick, index).start()

    for count in range(1, 4):

        @when(sector + count > last)
        def _():
            def clear(number, carry):
                slots[number // CHUNKS, number % CHUNKS, count] = jnp.zeros((rows, width), jnp.float32)
                return carry

            lax.fori_loop(0, ticks * CHUNKS, clear, 0)

    @when(site == last_site)
    def _():
        for tick in range(ticks - 1):
            for index in range(CHUNKS):
                entering_copy(tick, index).wait()

    steps = ticks * CHUNKS
    pass_on(0, 0)
    start(first_sends(AHEAD))

    for copy in small_copies:
        copy.wait()

    for number in range(1, CHUNKS - AHEAD):
        pass_on(0, number)
        start(first_sends(AHEAD + number))
    for number in range(CHUNKS - AHEAD, AHEAD):
        pass_on(0, number)

    def step(number, carry):
        tick, index = number // CHUNKS, number % CHUNKS
        later = number + AHEAD

        @when(index == 0)
        def _():
            begin(tick)

        def meanwhile():
            @when(later < steps)
            def _():
                pass_on(later // CHUNKS, later % CHUNKS)

        work(tick, index, meanwhile)

        @when((index == CHUNKS // 2 - 1) & (tick > 0))
        def _():
            middle(tick)

        @when(index == CHUNKS - 1)
        def _():
            end(tick)

        return carry

    lax.fori_loop(0, steps, step, 0)

    @when(site >= 1)
    def _():
        wait_for(along_y.at[ticks, pl.ds(0, side - 1)], y_sem.at[ticks])
        now_scale, now_log = advance_from(ticks)
        carried[ticks + 1, 2:3, :] = now_log
        carried[ticks + 1, 3:4, :] = now_scale
        scale[...] = column_of(now_scale)

    @when(site == 0)
    def _():
        carried[ticks + 1, 2:3, :] = carried[ticks, 2:3, :]
        carried[ticks + 1, 3:4, :] = carried[ticks, 3:4, :]

    for index in range(CHUNKS):
        finish(first_sends(index))

    def drain(number, carry):
        tick, index = number // CHUNKS, number % CHUNKS
        finish([(condition, copy) for condition, _, copy in relays(tick, index)])

        @when(tick < ticks - 1)
        def _():
            finish(next_sends(tick, index))

        return carry

    lax.fori_loop(0, steps, drain, 0)

    def drain_sums(tick, carry):
        @when(site < last_site)
        def _():
            wait_for(along_x.at[0], x_send_sem.at[tick])

        @when((age_at(tick) >= 1) & (site < last_site))
        def _():
            wait_for(along_y.at[0], y_send_sem.at[tick + 1])

        return carry

    lax.fori_loop(0, ticks - 1, drain_sums, 0)
    @when(site >= 1)
    def _():
        wait_for(along_y.at[0, pl.ds(0, side - 1)], y_send_sem.at[ticks])

    all_but_one = along_all.at[pl.ds(0, last)]
    wait_for(all_but_one, all_send_sem.at[0])
    wait_for(all_but_one, all_sem.at[0])
    last_sums = [along_all[of_sector] for of_sector in range(side * side)]
    while len(last_sums) > 1:
        last_sums = [one + other for one, other in zip(last_sums[::2], last_sums[1::2])]
    last_sums = last_sums[0]
    now_scale, now_log = advance(last_sums, carried[ticks + 1, 2:3, :], carried[ticks + 1, 3:4, :])
    logp_out[...] = now_log
    factor = scale[...] * column_of(now_scale)
    for index in range(CHUNKS):
        part = factor[index * rows : (index + 1) * rows]
        env_out[0, index * rows : (index + 1) * rows, :] = picked[ticks - 1, index] * jnp.concatenate([part] * tiles, axis=1)


def solution(mesh):
    sites, sectors = mesh.shape["site"], mesh.shape["sector"]
    side = int(round(sectors**0.5))

    def per_device(site_tensor, outcomes, in_flight, prior_logp, entering):
        ticks = outcomes.shape[0]
        _, counts, _, width, _ = site_tensor.shape
        rows = in_flight.shape[1] // CHUNKS
        vmem = pl.BlockSpec(memory_space=pltpu.VMEM)
        f32, dma = jnp.float32, pltpu.SemaphoreType.DMA
        return pl.pallas_call(
            functools.partial(kernel, ticks, side, sites, float(width * sectors)),
            name="chain",
            out_shape=(
                jax.ShapeDtypeStruct(in_flight.shape, f32),
                jax.ShapeDtypeStruct(prior_logp.shape, f32),
            ),
            in_specs=[pl.BlockSpec(memory_space=pltpu.HBM)] * 5,
            out_specs=(vmem, vmem),
            scratch_shapes=[
                pltpu.VMEM(outcomes.shape, jnp.int32),
                pltpu.VMEM(prior_logp.shape, f32),
                pltpu.VMEM((counts, width, width), f32),
                pltpu.VMEM((counts, width, width), jnp.bfloat16),
                pltpu.VMEM((counts, width, width), jnp.bfloat16),
                pltpu.VMEM((ticks, CHUNKS, counts + 1, rows, width), f32),
                pltpu.VMEM((ticks, CHUNKS, rows, width), f32),
                pltpu.VMEM((LANES, LANES), f32),
                pltpu.VMEM((LANES, LANES), f32),
                pltpu.VMEM((LANES, LANES), f32),
                pltpu.VMEM((LANES, LANES), f32),
                pltpu.VMEM((ticks + 2, 4, LANES), f32),
                pltpu.VMEM((ticks, 4, LANES), f32),
                pltpu.VMEM((ticks, side, 4, LANES), f32),
                pltpu.VMEM((ticks + 1, side, 4, LANES), f32),
                pltpu.VMEM((side * side, 4, LANES), f32),
                dma((counts,)),
                dma((2 + ticks * CHUNKS,)),
                dma((ticks, CHUNKS, counts + 1)),
                dma((ticks,)),
                dma((ticks + 1,)),
                dma((1,)),
                dma((7, ticks, CHUNKS)),
                dma((ticks,)),
                dma((ticks + 1,)),
                dma((1,)),
            ],
            compiler_params=pltpu.CompilerParams(
                collective_id=0, has_side_effects=True, vmem_limit_bytes=48 * 1024 * 1024
            ),
            cost_estimate=pl.CostEstimate(
                flops=6 * ticks * counts * rows * CHUNKS * width * width,
                bytes_accessed=4 * counts * width * width,
                transcendentals=0,
            ),
        )(
            *(
                pltpu.with_memory_space_constraint(array, pltpu.HBM)
                for array in (site_tensor, outcomes, in_flight, prior_logp, entering)
            )
        )

    return jax.shard_map(
        per_device,
        mesh=mesh,
        in_specs=(
            P("site", None, "sector", None, None),
            P(None, "site", None),
            P("site", None, "sector"),
            P("site", None),
            P(None, None, "sector"),
        ),
        out_specs=(P("site", None, "sector"), P("site", None)),
        check_vma=False,
    )
```

```python
import functools

import jax
import jax.numpy as jnp
from jax import lax
from jax.experimental import pallas as pl
from jax.experimental.pallas import tpu as pltpu
from jax.sharding import PartitionSpec as P

EPSILON = 1e-06
CHUNKS = 4
AHEAD = 2
LANES = 128
MESH = pl.DeviceIdType.MESH


def when(condition):
    return pl.when(condition)


def diagonal():
    lane = lax.broadcasted_iota(jnp.int32, (LANES, LANES), 1)
    row = lax.broadcasted_iota(jnp.int32, (LANES, LANES), 0)
    return lane == row


def column_of(vector):
    spread = jnp.where(diagonal(), jnp.broadcast_to(vector, (LANES, LANES)), 0.0)
    return jnp.broadcast_to(jnp.sum(spread, axis=1, keepdims=True), (LANES, LANES))


def sums_of_rows(value):
    spread = jnp.where(diagonal(), jnp.sum(value, axis=1, keepdims=True), 0.0)
    return jnp.sum(spread, axis=0, keepdims=True)


def halves(value):
    high = value.astype(jnp.bfloat16)
    return high, (value - high.astype(jnp.float32)).astype(jnp.bfloat16)


def kernel(
    ticks,
    side,
    sites,
    bond,
    site_tensor,
    outcomes_in,
    in_flight,
    prior_in,
    entering,
    env_out,
    logp_out,
    outcomes,
    prior,
    raw,
    high,
    low,
    slots,
    picked,
    chosen,
    scale,
    picked_fold,
    total_fold,
    carried,
    message,
    along_x,
    along_y,
    along_all,
    raw_sem,
    local_sem,
    slot_sem,
    x_sem,
    y_sem,
    all_sem,
    send_sem,
    x_send_sem,
    y_send_sem,
    all_send_sem,
):
    site, sector = lax.axis_index("site"), lax.axis_index("sector")
    x, y = sector % side, sector // side
    last = side * side - 1
    last_site = sites - 1
    next_site = (site + 1) % sites
    site_before = (site + sites - 1) % sites
    even = site % 2 == 0
    rows = slots.shape[3]
    width = slots.shape[4]
    tiles = width // LANES
    always = site >= 0

    raw_copies = [
        pltpu.make_async_copy(site_tensor.at[0, count, 0], raw.at[count], raw_sem.at[count]) for count in range(4)
    ]
    small_copies = [
        pltpu.make_async_copy(outcomes_in, outcomes, local_sem.at[0]),
        pltpu.make_async_copy(prior_in, prior, local_sem.at[1]),
    ]
    row_copies = [
        pltpu.make_async_copy(
            in_flight.at[0, pl.ds(index * rows, rows), :], slots.at[0, index, 0], slot_sem.at[0, index, 0]
        )
        for index in range(CHUNKS)
    ]

    def entering_copy(tick, index):
        return pltpu.make_async_copy(
            entering.at[tick, pl.ds(index * rows, rows), :], picked.at[tick, index], local_sem.at[2 + tick * CHUNKS + index]
        )

    barrier = pltpu.get_barrier_semaphore()
    expected = jnp.int32(0)

    def greet(from_condition, where, to_condition):
        @when(from_condition)
        def _():
            pl.semaphore_signal(barrier, inc=1, device_id=where, device_id_type=MESH)

        return to_condition.astype(jnp.int32)

    for hop in range(side):
        expected += greet(always, (site_before, y * side + (x + hop) % side), always)
    for hop in range(1, side):
        expected += greet(always, (site_before, (y + hop) % side * side + x), always)
    expected += greet((x == side - 1) & (sector < last), (site_before, sector + 1), (x == 0) & (sector > 0))
    expected += greet((x != 0) & (sector + 3 <= last), (site_before, sector + 3), (x != side - 1) & (sector >= 3))
    expected += greet(sector == last, (site_before, 0 * sector + 2), sector == 2)
    for hop in range(1, last + 1):
        expected += greet(always, (site, (sector + hop) % (last + 1)), always)

    for copy in row_copies + small_copies + raw_copies:
        copy.start()

    for count in range(4):
        raw_copies[count].wait()

        def cut(step, carry):
            part = pl.ds(pl.multiple_of(step * 64, 64), 64)
            high[count, part, :], low[count, part, :] = halves(raw[count, part, :])
            return carry

        lax.fori_loop(0, width // 64, cut, 0)

    pl.semaphore_wait(barrier, expected)

    def remote(source, tick, index, count, kind, where):
        return pltpu.make_async_remote_copy(
            src_ref=source,
            dst_ref=slots.at[tick, index, count],
            send_sem=send_sem.at[kind, tick, index],
            recv_sem=slot_sem.at[tick, index, count],
            device_id=where,
            device_id_type=MESH,
        )

    odd_to = next_site % 2 == 1

    def sends(source, tick, index, to_site, odd):
        first_column = odd & (x == 0)
        third_column = odd & (x == 2)
        to_left = (sector >= 1) & jnp.logical_not(first_column)
        left = remote(source, tick, index, 1, 0, (to_site, sector - 1))
        left_first = odd == (x >= 2)
        return [
            (to_left & left_first, left),
            ((sector >= 3) & jnp.logical_not(third_column), remote(source, tick, index, 3, 1, (to_site, sector - 3))),
            ((sector >= side) & (first_column | third_column), remote(source, tick, index, 4, 2, (to_site, sector - side))),
            ((sector == 2) & jnp.logical_not(odd), remote(source, tick, index, 4, 2, (to_site, last))),
            (to_left & jnp.logical_not(left_first), left),
        ]

    def first_sends(index):
        return sends(in_flight.at[0, pl.ds(index * rows, rows), :], 0, index, site, jnp.logical_not(even))

    def next_sends(tick, index):
        source = picked.at[tick, index]
        own = (always, remote(source, tick + 1, index, 0, 3, (next_site, sector)))
        return sends(source, tick + 1, index, next_site, odd_to) + [own]

    def by_left(of_sector):
        return even == (of_sector % side < 2)

    left_on = (sector + 1 <= last) & (sector >= 1) & by_left(sector + 1)
    right_on = (sector + 3 <= last) & jnp.logical_not(by_left(sector + 3))
    crossed = jnp.logical_not(even) & (sector + side <= last)
    stage_first, stage_third = crossed & (x == 0), crossed & (x == 2)
    stage_two = even & (sector == last)

    def relays(tick, index):
        stage, one, three = slots.at[tick, index, 4], slots.at[tick, index, 1], slots.at[tick, index, 3]
        return [
            (stage_first, 4, remote(stage, tick, index, 1, 4, (site, sector + 3))),
            (stage_third, 4, remote(stage, tick, index, 3, 4, (site, sector + 1))),
            (stage_two, 4, remote(stage, tick, index, 2, 4, (site, 0 * sector))),
            (left_on, 1, remote(one, tick, index, 2, 5, (site, sector - 1))),
            (right_on, 3, remote(three, tick, index, 2, 6, (site, sector + 1))),
        ]

    def start(copies):
        for condition, copy in copies:
            when(condition)(copy.start)

    def finish(copies):
        for condition, copy in copies:
            when(condition)(copy.wait_send)

    def arrived(tick, index, count):
        remote(slots.at[tick, index, count], tick, index, count, 0, (site, sector)).wait_recv()

    def x_sends(tick, to_site):
        return [
            pltpu.make_async_remote_copy(
                src_ref=message.at[tick],
                dst_ref=along_x.at[tick + 1, x],
                send_sem=x_send_sem.at[tick],
                recv_sem=x_sem.at[tick + 1],
                device_id=(to_site, y * side + (x + hop) % side),
                device_id_type=MESH,
            )
            for hop in range(side)
        ]

    def y_sends(slot, to_site):
        return [
            pltpu.make_async_remote_copy(
                src_ref=carried.at[slot],
                dst_ref=along_y.at[slot, y],
                send_sem=y_send_sem.at[slot],
                recv_sem=y_sem.at[slot],
                device_id=(to_site, (y + hop) % side * side + x),
                device_id_type=MESH,
            )
            for hop in range(side)
        ]

    def all_sends():
        return [
            pltpu.make_async_remote_copy(
                src_ref=message.at[ticks - 1],
                dst_ref=along_all.at[sector],
                send_sem=all_send_sem.at[0],
                recv_sem=all_sem.at[0],
                device_id=(site, (sector + hop) % (last + 1)),
                device_id_type=MESH,
            )
            for hop in range(1, last + 1)
        ]

    def wait_for(ref, sem):
        pltpu.make_async_copy(ref, ref, sem).wait()

    def four(ref, tick):
        return (ref[tick, 0] + ref[tick, 1]) + (ref[tick, 2] + ref[tick, 3])

    def advance(sums, before_log, before_scale):
        picked_power = sums[0:1] * before_scale * before_scale / bond + EPSILON
        total_power = sums[1:2] * before_scale * before_scale / bond + EPSILON
        return 1.0 / jnp.sqrt(picked_power), before_log + jnp.log(picked_power) - jnp.log(total_power)

    def advance_from(slot):
        before = along_y[slot, 0]
        return advance(four(along_y, slot), before[2:3], before[3:4])

    def age_at(tick):
        return jnp.minimum(tick, site)

    def begin(tick):
        age = age_at(tick)
        chosen[...] = column_of(outcomes[tick].astype(jnp.float32))

        @when(age >= 2)
        def _():
            wait_for(along_y.at[tick], y_sem.at[tick])
            now_scale, now_log = advance_from(tick)
            carried[tick + 1, 2:3, :] = now_log
            carried[tick + 1, 3:4, :] = now_scale
            scale[...] = column_of(now_scale)

        @when(age < 2)
        def _():
            carried[tick + 1, 2:3, :] = jnp.where(tick == 0, prior[...], 0.0)
            carried[tick + 1, 3:4, :] = jnp.ones((1, LANES), jnp.float32)
            scale[...] = jnp.ones((LANES, LANES), jnp.float32)

    def middle(tick):
        @when(age_at(tick) >= 1)
        def _():
            wait_for(along_x.at[tick], x_sem.at[tick])
            sums = four(along_x, tick)
            carried[tick + 1, 0:2, :] = sums[0:2]

            @when(age_at(tick) == 1)
            def _():
                carried[tick + 1, 2:3, :] = along_x[tick, 0][2:3]

            @when((tick < ticks - 1) & (site < last_site))
            def _():
                for copy in y_sends(tick + 1, next_site):
                    copy.start()

            @when(tick == ticks - 1)
            def _():
                for copy in y_sends(ticks, site)[1:]:
                    copy.start()
                along_y[ticks, y] = carried[ticks]

    def end(tick):
        message[tick, 0:1, :] = sums_of_rows(picked_fold[...])
        message[tick, 1:2, :] = sums_of_rows(total_fold[...])
        message[tick, 2:3, :] = carried[tick + 1, 2:3, :]
        message[tick, 3:4, :] = carried[tick + 1, 3:4, :]

        @when((tick < ticks - 1) & (site < last_site))
        def _():
            for copy in x_sends(tick, next_site):
                copy.start()

        @when(tick == ticks - 1)
        def _():
            for copy in all_sends():
                copy.start()
            along_all[sector] = message[ticks - 1]

    def pass_on(tick, index):
        for condition, count, copy in relays(tick, index):

            @when(condition)
            def _():
                arrived(tick, index, count)
                copy.start()

    def work(tick, index, meanwhile):
        @when(tick == 0)
        def _():
            wait_for(slots.at[0, index, 0], slot_sem.at[0, index, 0])

        @when(tick > 0)
        def _():
            arrived(tick, index, 0)

        part = pl.ds(pl.multiple_of(index * rows, rows), rows)
        factor = jnp.concatenate([scale[part, :]] * tiles, axis=1)
        choice = jnp.concatenate([chosen[part, :]] * tiles, axis=1)
        selected = jnp.zeros((rows, width), jnp.float32)
        squares = jnp.zeros((rows, width), jnp.float32)
        for count in (0, 1, 3, 2):
            if count == 1:
                when((sector + 1 <= last) & jnp.logical_not(left_on))(lambda: arrived(tick, index, 1))
                when((sector + 3 <= last) & jnp.logical_not(right_on))(lambda: arrived(tick, index, 3))
            if count == 2:
                meanwhile()
                when(sector + 2 <= last)(lambda: arrived(tick, index, 2))
            block_high, block_low = halves(slots[tick, index, count])
            both = jnp.dot(
                jnp.concatenate([block_high, block_low], axis=0), high[count], preferred_element_type=jnp.float32
            )
            rest = jnp.dot(block_high, low[count], preferred_element_type=jnp.float32)
            amplitude = (both[:rows] + (both[rows:] + rest)) * factor
            selected = jnp.where(choice == float(count), amplitude, selected)
            squares = squares + amplitude * amplitude

        @when((site < last_site) | (tick == ticks - 1))
        def _():
            picked[tick, index] = selected

        @when(tick < ticks - 1)
        def _():
            start(next_sends(tick, index))

        def folded(value):
            return sum(value[:, tile * LANES : (tile + 1) * LANES] for tile in range(tiles))

        picked_fold[part, :] = folded(selected * selected)
        total_fold[part, :] = folded(squares)

    for index in range(AHEAD):
        start(first_sends(index))

    @when(site == last_site)
    def _():
        for tick in range(ticks - 1):
            for index in range(CHUNKS):
                entering_copy(tick, index).start()

    for count in range(1, 4):

        @when(sector + count > last)
        def _():
            def clear(number, carry):
                slots[number // CHUNKS, number % CHUNKS, count] = jnp.zeros((rows, width), jnp.float32)
                return carry

            lax.fori_loop(0, ticks * CHUNKS, clear, 0)

    @when(site == last_site)
    def _():
        for tick in range(ticks - 1):
            for index in range(CHUNKS):
                entering_copy(tick, index).wait()

    steps = ticks * CHUNKS
    pass_on(0, 0)
    start(first_sends(AHEAD))

    for copy in small_copies:
        copy.wait()

    for number in range(1, CHUNKS - AHEAD):
        pass_on(0, number)
        start(first_sends(AHEAD + number))
    for number in range(CHUNKS - AHEAD, AHEAD):
        pass_on(0, number)

    def drain(number, carry):
        tick, index = number // CHUNKS, number % CHUNKS
        finish([(condition, copy) for condition, _, copy in relays(tick, index)])

        @when(tick < ticks - 1)
        def _():
            finish(next_sends(tick, index))

        return carry

    lag = 2 * CHUNKS

    def step(number, carry):
        tick, index = number // CHUNKS, number % CHUNKS
        later = number + AHEAD

        @when(index == 0)
        def _():
            begin(tick)

        def meanwhile():
            @when(later < steps)
            def _():
                pass_on(later // CHUNKS, later % CHUNKS)

        work(tick, index, meanwhile)

        @when(number >= lag)
        def _():
            drain(number - lag, 0)

        @when((index == CHUNKS // 2 - 1) & (tick > 0))
        def _():
            middle(tick)

        @when(index == CHUNKS - 1)
        def _():
            end(tick)

        return carry

    lax.fori_loop(0, steps, step, 0)

    @when(site >= 1)
    def _():
        wait_for(along_y.at[ticks, pl.ds(0, side - 1)], y_sem.at[ticks])
        now_scale, now_log = advance_from(ticks)
        carried[ticks + 1, 2:3, :] = now_log
        carried[ticks + 1, 3:4, :] = now_scale
        scale[...] = column_of(now_scale)

    @when(site == 0)
    def _():
        carried[ticks + 1, 2:3, :] = carried[ticks, 2:3, :]
        carried[ticks + 1, 3:4, :] = carried[ticks, 3:4, :]

    for index in range(CHUNKS):
        finish(first_sends(index))

    lax.fori_loop(steps - lag, steps, drain, 0)

    def drain_sums(tick, carry):
        @when(site < last_site)
        def _():
            wait_for(along_x.at[0], x_send_sem.at[tick])

        @when((age_at(tick) >= 1) & (site < last_site))
        def _():
            wait_for(along_y.at[0], y_send_sem.at[tick + 1])

        return carry

    lax.fori_loop(0, ticks - 1, drain_sums, 0)
    @when(site >= 1)
    def _():
        wait_for(along_y.at[0, pl.ds(0, side - 1)], y_send_sem.at[ticks])

    all_but_one = along_all.at[pl.ds(0, last)]
    wait_for(all_but_one, all_send_sem.at[0])
    wait_for(all_but_one, all_sem.at[0])
    last_sums = [along_all[of_sector] for of_sector in range(side * side)]
    while len(last_sums) > 1:
        last_sums = [one + other for one, other in zip(last_sums[::2], last_sums[1::2])]
    last_sums = last_sums[0]
    now_scale, now_log = advance(last_sums, carried[ticks + 1, 2:3, :], carried[ticks + 1, 3:4, :])
    logp_out[...] = now_log
    factor = scale[...] * column_of(now_scale)
    for index in range(CHUNKS):
        part = factor[index * rows : (index + 1) * rows]
        env_out[0, index * rows : (index + 1) * rows, :] = picked[ticks - 1, index] * jnp.concatenate([part] * tiles, axis=1)


def solution(mesh):
    sites, sectors = mesh.shape["site"], mesh.shape["sector"]
    side = int(round(sectors**0.5))

    def per_device(site_tensor, outcomes, in_flight, prior_logp, entering):
        ticks = outcomes.shape[0]
        _, counts, _, width, _ = site_tensor.shape
        rows = in_flight.shape[1] // CHUNKS
        vmem = pl.BlockSpec(memory_space=pltpu.VMEM)
        f32, dma = jnp.float32, pltpu.SemaphoreType.DMA
        return pl.pallas_call(
            functools.partial(kernel, ticks, side, sites, float(width * sectors)),
            name="chain",
            out_shape=(
                jax.ShapeDtypeStruct(in_flight.shape, f32),
                jax.ShapeDtypeStruct(prior_logp.shape, f32),
            ),
            in_specs=[pl.BlockSpec(memory_space=pltpu.HBM)] * 5,
            out_specs=(vmem, vmem),
            scratch_shapes=[
                pltpu.VMEM(outcomes.shape, jnp.int32),
                pltpu.VMEM(prior_logp.shape, f32),
                pltpu.VMEM((counts, width, width), f32),
                pltpu.VMEM((counts, width, width), jnp.bfloat16),
                pltpu.VMEM((counts, width, width), jnp.bfloat16),
                pltpu.VMEM((ticks, CHUNKS, counts + 1, rows, width), f32),
                pltpu.VMEM((ticks, CHUNKS, rows, width), f32),
                pltpu.VMEM((LANES, LANES), f32),
                pltpu.VMEM((LANES, LANES), f32),
                pltpu.VMEM((LANES, LANES), f32),
                pltpu.VMEM((LANES, LANES), f32),
                pltpu.VMEM((ticks + 2, 4, LANES), f32),
                pltpu.VMEM((ticks, 4, LANES), f32),
                pltpu.VMEM((ticks, side, 4, LANES), f32),
                pltpu.VMEM((ticks + 1, side, 4, LANES), f32),
                pltpu.VMEM((side * side, 4, LANES), f32),
                dma((counts,)),
                dma((2 + ticks * CHUNKS,)),
                dma((ticks, CHUNKS, counts + 1)),
                dma((ticks,)),
                dma((ticks + 1,)),
                dma((1,)),
                dma((7, ticks, CHUNKS)),
                dma((ticks,)),
                dma((ticks + 1,)),
                dma((1,)),
            ],
            compiler_params=pltpu.CompilerParams(
                collective_id=0, has_side_effects=True, vmem_limit_bytes=48 * 1024 * 1024
            ),
            cost_estimate=pl.CostEstimate(
                flops=6 * ticks * counts * rows * CHUNKS * width * width,
                bytes_accessed=4 * counts * width * width,
                transcendentals=0,
            ),
        )(
            *(
                pltpu.with_memory_space_constraint(array, pltpu.HBM)
                for array in (site_tensor, outcomes, in_flight, prior_logp, entering)
            )
        )

    return jax.shard_map(
        per_device,
        mesh=mesh,
        in_specs=(
            P("site", None, "sector", None, None),
            P(None, "site", None),
            P("site", None, "sector"),
            P("site", None),
            P(None, None, "sector"),
        ),
        out_specs=(P("site", None, "sector"), P("site", None)),
        check_vma=False,
    )
```

```python
import functools

import jax
import jax.numpy as jnp
from jax import lax
from jax.experimental import pallas as pl
from jax.experimental.pallas import tpu as pltpu
from jax.sharding import PartitionSpec as P

EPSILON = 1e-06
CHUNKS = 4
AHEAD = 2
LANES = 128
MESH = pl.DeviceIdType.MESH


def when(condition):
    return pl.when(condition)


def diagonal():
    lane = lax.broadcasted_iota(jnp.int32, (LANES, LANES), 1)
    row = lax.broadcasted_iota(jnp.int32, (LANES, LANES), 0)
    return lane == row


def column_of(vector):
    spread = jnp.where(diagonal(), jnp.broadcast_to(vector, (LANES, LANES)), 0.0)
    return jnp.broadcast_to(jnp.sum(spread, axis=1, keepdims=True), (LANES, LANES))


def sums_of_rows(value):
    spread = jnp.where(diagonal(), jnp.sum(value, axis=1, keepdims=True), 0.0)
    return jnp.sum(spread, axis=0, keepdims=True)


def halves(value):
    high = value.astype(jnp.bfloat16)
    return high, (value - high.astype(jnp.float32)).astype(jnp.bfloat16)


def kernel(
    ticks,
    side,
    sites,
    bond,
    site_tensor,
    outcomes_in,
    in_flight,
    prior_in,
    entering,
    env_out,
    logp_out,
    outcomes,
    prior,
    raw,
    high,
    low,
    slots,
    picked,
    chosen,
    scale,
    picked_fold,
    total_fold,
    carried,
    message,
    along_x,
    along_y,
    along_all,
    raw_sem,
    local_sem,
    slot_sem,
    x_sem,
    y_sem,
    all_sem,
    send_sem,
    x_send_sem,
    y_send_sem,
    all_send_sem,
):
    site, sector = lax.axis_index("site"), lax.axis_index("sector")
    x, y = sector % side, sector // side
    last = side * side - 1
    last_site = sites - 1
    next_site = (site + 1) % sites
    site_before = (site + sites - 1) % sites
    even = site % 2 == 0
    rows = slots.shape[3]
    width = slots.shape[4]
    tiles = width // LANES
    always = site >= 0

    raw_copies = [
        pltpu.make_async_copy(site_tensor.at[0, count, 0], raw.at[count], raw_sem.at[count]) for count in range(4)
    ]
    small_copies = [
        pltpu.make_async_copy(outcomes_in, outcomes, local_sem.at[0]),
        pltpu.make_async_copy(prior_in, prior, local_sem.at[1]),
    ]
    row_copies = [
        pltpu.make_async_copy(
            in_flight.at[0, pl.ds(index * rows, rows), :], slots.at[0, index, 0], slot_sem.at[0, index, 0]
        )
        for index in range(CHUNKS)
    ]

    def entering_copy(tick, index):
        return pltpu.make_async_copy(
            entering.at[tick, pl.ds(index * rows, rows), :], picked.at[tick, index], local_sem.at[2 + tick * CHUNKS + index]
        )

    barrier = pltpu.get_barrier_semaphore()
    expected = jnp.int32(0)

    def greet(from_condition, where, to_condition):
        @when(from_condition)
        def _():
            pl.semaphore_signal(barrier, inc=1, device_id=where, device_id_type=MESH)

        return to_condition.astype(jnp.int32)

    for hop in range(side):
        expected += greet(always, (site_before, y * side + (x + hop) % side), always)
    for hop in range(1, side):
        expected += greet(always, (site_before, (y + hop) % side * side + x), always)
    expected += greet((x == side - 1) & (sector < last), (site_before, sector + 1), (x == 0) & (sector > 0))
    expected += greet((x != 0) & (sector + 3 <= last), (site_before, sector + 3), (x != side - 1) & (sector >= 3))
    expected += greet(sector == last, (site_before, 0 * sector + 2), sector == 2)
    for hop in range(1, last + 1):
        expected += greet(always, (site, (sector + hop) % (last + 1)), always)

    for copy in row_copies + small_copies + raw_copies:
        copy.start()

    for count in range(4):
        raw_copies[count].wait()

        def cut(step, carry):
            part = pl.ds(pl.multiple_of(step * 64, 64), 64)
            high[count, part, :], low[count, part, :] = halves(raw[count, part, :])
            return carry

        lax.fori_loop(0, width // 64, cut, 0)

    pl.semaphore_wait(barrier, expected)

    def remote(source, tick, index, count, kind, where):
        return pltpu.make_async_remote_copy(
            src_ref=source,
            dst_ref=slots.at[tick, index, count],
            send_sem=send_sem.at[kind, tick, index],
            recv_sem=slot_sem.at[tick, index, count],
            device_id=where,
            device_id_type=MESH,
        )

    odd_to = next_site % 2 == 1

    def sends(source, tick, index, to_site, odd):
        first_column = odd & (x == 0)
        third_column = odd & (x == 2)
        to_left = (sector >= 1) & jnp.logical_not(first_column)
        left = remote(source, tick, index, 1, 0, (to_site, sector - 1))
        left_first = odd == (x >= 2)
        return [
            (to_left & left_first, left),
            ((sector >= 3) & jnp.logical_not(third_column), remote(source, tick, index, 3, 1, (to_site, sector - 3))),
            ((sector >= side) & (first_column | third_column), remote(source, tick, index, 4, 2, (to_site, sector - side))),
            ((sector == 2) & jnp.logical_not(odd), remote(source, tick, index, 4, 2, (to_site, last))),
            (to_left & jnp.logical_not(left_first), left),
        ]

    def first_sends(index):
        return sends(in_flight.at[0, pl.ds(index * rows, rows), :], 0, index, site, jnp.logical_not(even))

    def next_sends(tick, index):
        source = picked.at[tick, index]
        own = (always, remote(source, tick + 1, index, 0, 3, (next_site, sector)))
        return sends(source, tick + 1, index, next_site, odd_to) + [own]

    def by_left(of_sector):
        return even == (of_sector % side < 2)

    left_on = (sector + 1 <= last) & (sector >= 1) & by_left(sector + 1)
    right_on = (sector + 3 <= last) & jnp.logical_not(by_left(sector + 3))
    crossed = jnp.logical_not(even) & (sector + side <= last)
    stage_first, stage_third = crossed & (x == 0), crossed & (x == 2)
    stage_two = even & (sector == last)

    def relays(tick, index):
        stage, one, three = slots.at[tick, index, 4], slots.at[tick, index, 1], slots.at[tick, index, 3]
        return [
            (stage_first, 4, remote(stage, tick, index, 1, 4, (site, sector + 3))),
            (stage_third, 4, remote(stage, tick, index, 3, 4, (site, sector + 1))),
            (stage_two, 4, remote(stage, tick, index, 2, 4, (site, 0 * sector))),
            (left_on, 1, remote(one, tick, index, 2, 5, (site, sector - 1))),
            (right_on, 3, remote(three, tick, index, 2, 6, (site, sector + 1))),
        ]

    def start(copies):
        for condition, copy in copies:
            when(condition)(copy.start)

    def finish(copies):
        for condition, copy in copies:
            when(condition)(copy.wait_send)

    def arrived(tick, index, count):
        remote(slots.at[tick, index, count], tick, index, count, 0, (site, sector)).wait_recv()

    def x_sends(tick, to_site):
        return [
            pltpu.make_async_remote_copy(
                src_ref=message.at[tick],
                dst_ref=along_x.at[tick + 1, x],
                send_sem=x_send_sem.at[tick],
                recv_sem=x_sem.at[tick + 1],
                device_id=(to_site, y * side + (x + hop) % side),
                device_id_type=MESH,
            )
            for hop in range(side)
        ]

    def y_sends(slot, to_site):
        return [
            pltpu.make_async_remote_copy(
                src_ref=carried.at[slot],
                dst_ref=along_y.at[slot, y],
                send_sem=y_send_sem.at[slot],
                recv_sem=y_sem.at[slot],
                device_id=(to_site, (y + hop) % side * side + x),
                device_id_type=MESH,
            )
            for hop in range(side)
        ]

    def all_sends():
        return [
            pltpu.make_async_remote_copy(
                src_ref=message.at[ticks - 1],
                dst_ref=along_all.at[sector],
                send_sem=all_send_sem.at[0],
                recv_sem=all_sem.at[0],
                device_id=(site, (sector + hop) % (last + 1)),
                device_id_type=MESH,
            )
            for hop in range(1, last + 1)
        ]

    def wait_for(ref, sem):
        pltpu.make_async_copy(ref, ref, sem).wait()

    def four(ref, tick):
        return (ref[tick, 0] + ref[tick, 1]) + (ref[tick, 2] + ref[tick, 3])

    def advance(sums, before_log, before_scale):
        picked_power = sums[0:1] * before_scale * before_scale / bond + EPSILON
        total_power = sums[1:2] * before_scale * before_scale / bond + EPSILON
        return 1.0 / jnp.sqrt(picked_power), before_log + jnp.log(picked_power) - jnp.log(total_power)

    def advance_from(slot):
        before = along_y[slot, 0]
        return advance(four(along_y, slot), before[2:3], before[3:4])

    def age_at(tick):
        return jnp.minimum(tick, site)

    def begin(tick):
        age = age_at(tick)
        chosen[...] = column_of(outcomes[tick].astype(jnp.float32))

        @when(age >= 2)
        def _():
            wait_for(along_y.at[tick], y_sem.at[tick])
            now_scale, now_log = advance_from(tick)
            carried[tick + 1, 2:3, :] = now_log
            carried[tick + 1, 3:4, :] = now_scale
            scale[...] = column_of(now_scale)

        @when(age < 2)
        def _():
            carried[tick + 1, 2:3, :] = jnp.where(tick == 0, prior[...], 0.0)
            carried[tick + 1, 3:4, :] = jnp.ones((1, LANES), jnp.float32)
            scale[...] = jnp.ones((LANES, LANES), jnp.float32)

    def middle(tick):
        @when(age_at(tick) >= 1)
        def _():
            wait_for(along_x.at[tick], x_sem.at[tick])
            sums = four(along_x, tick)
            carried[tick + 1, 0:2, :] = sums[0:2]

            @when(age_at(tick) == 1)
            def _():
                carried[tick + 1, 2:3, :] = along_x[tick, 0][2:3]

            @when((tick < ticks - 1) & (site < last_site))
            def _():
                for copy in y_sends(tick + 1, next_site):
                    copy.start()

            @when(tick == ticks - 1)
            def _():
                for copy in y_sends(ticks, site)[1:]:
                    copy.start()
                along_y[ticks, y] = carried[ticks]

    def end(tick):
        message[tick, 0:1, :] = sums_of_rows(picked_fold[...])
        message[tick, 1:2, :] = sums_of_rows(total_fold[...])
        message[tick, 2:3, :] = carried[tick + 1, 2:3, :]
        message[tick, 3:4, :] = carried[tick + 1, 3:4, :]

        @when((tick < ticks - 1) & (site < last_site))
        def _():
            for copy in x_sends(tick, next_site):
                copy.start()

        @when(tick == ticks - 1)
        def _():
            for copy in all_sends():
                copy.start()
            along_all[sector] = message[ticks - 1]

    def pass_on(tick, index):
        for condition, count, copy in relays(tick, index):

            @when(condition)
            def _():
                arrived(tick, index, count)
                copy.start()

    def work(tick, index, meanwhile):
        @when(tick == 0)
        def _():
            wait_for(slots.at[0, index, 0], slot_sem.at[0, index, 0])

        @when(tick > 0)
        def _():
            arrived(tick, index, 0)

        part = pl.ds(pl.multiple_of(index * rows, rows), rows)
        products = []
        for count in (0, 1, 3, 2):
            if count == 1:
                when((sector + 1 <= last) & jnp.logical_not(left_on))(lambda: arrived(tick, index, 1))
                when((sector + 3 <= last) & jnp.logical_not(right_on))(lambda: arrived(tick, index, 3))
            if count == 2:
                meanwhile()
                when(sector + 2 <= last)(lambda: arrived(tick, index, 2))
            block_high, block_low = halves(slots[tick, index, count])
            both = jnp.dot(
                jnp.concatenate([block_high, block_low], axis=0), high[count], preferred_element_type=jnp.float32
            )
            rest = jnp.dot(block_high, low[count], preferred_element_type=jnp.float32)
            product = both[:rows] + (both[rows:] + rest)
            products.append((count, product))

        @when(index == 0)
        def _():
            begin(tick)

        factor = jnp.concatenate([scale[part, :]] * tiles, axis=1)
        choice = jnp.concatenate([chosen[part, :]] * tiles, axis=1)
        selected = jnp.zeros((rows, width), jnp.float32)
        squares = jnp.zeros((rows, width), jnp.float32)
        for count, product in products:
            amplitude = product * factor
            selected = jnp.where(choice == float(count), amplitude, selected)
            squares = squares + amplitude * amplitude

        @when((site < last_site) | (tick == ticks - 1))
        def _():
            picked[tick, index] = selected

        @when(tick < ticks - 1)
        def _():
            start(next_sends(tick, index))

        def folded(value):
            return sum(value[:, tile * LANES : (tile + 1) * LANES] for tile in range(tiles))

        picked_fold[part, :] = folded(selected * selected)
        total_fold[part, :] = folded(squares)

    for index in range(AHEAD):
        start(first_sends(index))

    @when(site == last_site)
    def _():
        for tick in range(ticks - 1):
            for index in range(CHUNKS):
                entering_copy(tick, index).start()

    for count in range(1, 4):

        @when(sector + count > last)
        def _():
            def clear(number, carry):
                slots[number // CHUNKS, number % CHUNKS, count] = jnp.zeros((rows, width), jnp.float32)
                return carry

            lax.fori_loop(0, ticks * CHUNKS, clear, 0)

    @when(site == last_site)
    def _():
        for tick in range(ticks - 1):
            for index in range(CHUNKS):
                entering_copy(tick, index).wait()

    steps = ticks * CHUNKS
    pass_on(0, 0)
    start(first_sends(AHEAD))

    for copy in small_copies:
        copy.wait()

    for number in range(1, CHUNKS - AHEAD):
        pass_on(0, number)
        start(first_sends(AHEAD + number))
    for number in range(CHUNKS - AHEAD, AHEAD):
        pass_on(0, number)

    def step(number, carry):
        tick, index = number // CHUNKS, number % CHUNKS
        later = number + AHEAD

        def meanwhile():
            @when(later < steps)
            def _():
                pass_on(later // CHUNKS, later % CHUNKS)

        work(tick, index, meanwhile)

        @when((index == CHUNKS // 2 - 1) & (tick > 0))
        def _():
            middle(tick)

        @when(index == CHUNKS - 1)
        def _():
            end(tick)

        return carry

    lax.fori_loop(0, steps, step, 0)

    @when(site >= 1)
    def _():
        wait_for(along_y.at[ticks, pl.ds(0, side - 1)], y_sem.at[ticks])
        now_scale, now_log = advance_from(ticks)
        carried[ticks + 1, 2:3, :] = now_log
        carried[ticks + 1, 3:4, :] = now_scale
        scale[...] = column_of(now_scale)

    @when(site == 0)
    def _():
        carried[ticks + 1, 2:3, :] = carried[ticks, 2:3, :]
        carried[ticks + 1, 3:4, :] = carried[ticks, 3:4, :]

    for index in range(CHUNKS):
        finish(first_sends(index))

    def drain(number, carry):
        tick, index = number // CHUNKS, number % CHUNKS
        finish([(condition, copy) for condition, _, copy in relays(tick, index)])

        @when(tick < ticks - 1)
        def _():
            finish(next_sends(tick, index))

        return carry

    lax.fori_loop(0, steps, drain, 0)

    def drain_sums(tick, carry):
        @when(site < last_site)
        def _():
            wait_for(along_x.at[0], x_send_sem.at[tick])

        @when((age_at(tick) >= 1) & (site < last_site))
        def _():
            wait_for(along_y.at[0], y_send_sem.at[tick + 1])

        return carry

    lax.fori_loop(0, ticks - 1, drain_sums, 0)
    @when(site >= 1)
    def _():
        wait_for(along_y.at[0, pl.ds(0, side - 1)], y_send_sem.at[ticks])

    all_but_one = along_all.at[pl.ds(0, last)]
    wait_for(all_but_one, all_send_sem.at[0])
    wait_for(all_but_one, all_sem.at[0])
    last_sums = [along_all[of_sector] for of_sector in range(side * side)]
    while len(last_sums) > 1:
        last_sums = [one + other for one, other in zip(last_sums[::2], last_sums[1::2])]
    last_sums = last_sums[0]
    now_scale, now_log = advance(last_sums, carried[ticks + 1, 2:3, :], carried[ticks + 1, 3:4, :])
    logp_out[...] = now_log
    factor = scale[...] * column_of(now_scale)
    for index in range(CHUNKS):
        part = factor[index * rows : (index + 1) * rows]
        env_out[0, index * rows : (index + 1) * rows, :] = picked[ticks - 1, index] * jnp.concatenate([part] * tiles, axis=1)


def solution(mesh):
    sites, sectors = mesh.shape["site"], mesh.shape["sector"]
    side = int(round(sectors**0.5))

    def per_device(site_tensor, outcomes, in_flight, prior_logp, entering):
        ticks = outcomes.shape[0]
        _, counts, _, width, _ = site_tensor.shape
        rows = in_flight.shape[1] // CHUNKS
        vmem = pl.BlockSpec(memory_space=pltpu.VMEM)
        f32, dma = jnp.float32, pltpu.SemaphoreType.DMA
        return pl.pallas_call(
            functools.partial(kernel, ticks, side, sites, float(width * sectors)),
            name="chain",
            out_shape=(
                jax.ShapeDtypeStruct(in_flight.shape, f32),
                jax.ShapeDtypeStruct(prior_logp.shape, f32),
            ),
            in_specs=[pl.BlockSpec(memory_space=pltpu.HBM)] * 5,
            out_specs=(vmem, vmem),
            scratch_shapes=[
                pltpu.VMEM(outcomes.shape, jnp.int32),
                pltpu.VMEM(prior_logp.shape, f32),
                pltpu.VMEM((counts, width, width), f32),
                pltpu.VMEM((counts, width, width), jnp.bfloat16),
                pltpu.VMEM((counts, width, width), jnp.bfloat16),
                pltpu.VMEM((ticks, CHUNKS, counts + 1, rows, width), f32),
                pltpu.VMEM((ticks, CHUNKS, rows, width), f32),
                pltpu.VMEM((LANES, LANES), f32),
                pltpu.VMEM((LANES, LANES), f32),
                pltpu.VMEM((LANES, LANES), f32),
                pltpu.VMEM((LANES, LANES), f32),
                pltpu.VMEM((ticks + 2, 4, LANES), f32),
                pltpu.VMEM((ticks, 4, LANES), f32),
                pltpu.VMEM((ticks, side, 4, LANES), f32),
                pltpu.VMEM((ticks + 1, side, 4, LANES), f32),
                pltpu.VMEM((side * side, 4, LANES), f32),
                dma((counts,)),
                dma((2 + ticks * CHUNKS,)),
                dma((ticks, CHUNKS, counts + 1)),
                dma((ticks,)),
                dma((ticks + 1,)),
                dma((1,)),
                dma((7, ticks, CHUNKS)),
                dma((ticks,)),
                dma((ticks + 1,)),
                dma((1,)),
            ],
            compiler_params=pltpu.CompilerParams(
                collective_id=0, has_side_effects=True, vmem_limit_bytes=48 * 1024 * 1024
            ),
            cost_estimate=pl.CostEstimate(
                flops=6 * ticks * counts * rows * CHUNKS * width * width,
                bytes_accessed=4 * counts * width * width,
                transcendentals=0,
            ),
        )(
            *(
                pltpu.with_memory_space_constraint(array, pltpu.HBM)
                for array in (site_tensor, outcomes, in_flight, prior_logp, entering)
            )
        )

    return jax.shard_map(
        per_device,
        mesh=mesh,
        in_specs=(
            P("site", None, "sector", None, None),
            P(None, "site", None),
            P("site", None, "sector"),
            P("site", None),
            P(None, None, "sector"),
        ),
        out_specs=(P("site", None, "sector"), P("site", None)),
        check_vma=False,
    )
```
